256 devices in a mesh: dp: 64 (over y_lo, x, z), tensor: 4 (over y_hi, core).
Axes of the slice: x: 4, y: 4 (y_hi: 2, y_lo: 2; y = y_hi * 2 + y_lo), z: 8, core: 2. Of those that a mesh axis runs over, the one named last changes fastest.
Arguments:
- tokens: bfloat16 [512, 3072], P(('dp', 'tensor')), may hold values from -6 to 6
- target: bfloat16 [512, 3072], P(('dp', 'tensor')), may hold values from -6 to 6
- master_up: float32 [24576, 3072], P(('dp', 'tensor')), may hold values from -0.109375 to 0.109375
- master_down: float32 [24576, 3072], P(('dp', 'tensor')), may hold values from -0.0390625 to 0.0390625
- tangent_up: bfloat16 [24576, 3072], P(('dp', 'tensor')), may hold values from -5 to 5
- tangent_down: bfloat16 [24576, 3072], P(('dp', 'tensor')), may hold values from -5 to 5
- moment_up: bfloat16 [24576, 3072], P(('dp', 'tensor')), may hold values from -0.15625 to 0.15625
- moment_down: bfloat16 [24576, 3072], P(('dp', 'tensor')), may hold values from -0.15625 to 0.15625
- curve_up: bfloat16 [24576, 3072], P(('dp', 'tensor')), may hold values from 0.19921875 to 4
- curve_down: bfloat16 [24576, 3072], P(('dp', 'tensor')), may hold values from 0.19921875 to 4
Outputs:
- step_up: float32 [24576, 3072], P(('dp', 'tensor'))
- step_down: float32 [24576, 3072], P(('dp', 'tensor'))
- moment_up_next: bfloat16 [24576, 3072], P(('dp', 'tensor'))
- moment_down_next: bfloat16 [24576, 3072], P(('dp', 'tensor'))
- curve_up_next: bfloat16 [24576, 3072], P(('dp', 'tensor'))
- curve_down_next: bfloat16 [24576, 3072], P(('dp', 'tensor'))
The draws below stay inside these ranges and needn't reach their ends.
All inputs are finite; a program needn't handle non-finite values.
Results may differ from the reference program's by a relative error of at most 0.009.
Values may be sent and summed in bfloat16 or wider, within the bound.
A program may use at most 128 MiB of HBM per device.

```python
import math
import jax
import jax.numpy as jnp
from jax import lax

D = 3072
FF = 24576
TOKENS = 512


def levels(own_key, shape, pieces, least, high):
    factor_of, own = 1.0, jax.random.fold_in(own_key, 6)
    for axis_at, parts in pieces:
        steps = jnp.exp(jax.random.uniform(jax.random.fold_in(own, axis_at), (parts,), jnp.float32, least / len(pieces), high / len(pieces)))
        factor_of = factor_of * jnp.repeat(steps, shape[axis_at] // parts).reshape([-1 if axis == axis_at else 1 for axis in range(len(shape))])
    return factor_of


def gaussian(key, shape, width, limit, split=(), kind=jnp.bfloat16):
    result = width * jax.random.normal(key, shape, jnp.float32)
    if split:
        result = result * levels(key, shape, split, -0.22, 0.18)
    return jnp.clip(result, -limit, limit).astype(kind)


def setup_inputs(seed: int = 0) -> dict:
    keys = jax.random.split(jax.random.key(seed), 11)
    return {
        "tokens": gaussian(keys[0], (TOKENS, D), 1.0, 6.0, ((0, 256),)),
        "target": gaussian(keys[1], (TOKENS, D), 1.0, 6.0, ((0, 256),)),
        "master_up": gaussian(keys[2], (FF, D), D ** -0.5, 0.109375, ((0, 256),), jnp.float32),
        "master_down": gaussian(keys[3], (FF, D), FF ** -0.5, 0.0390625, ((0, 256),), jnp.float32),
        "tangent_up": gaussian(keys[4], (FF, D), 1.0, 5.0, ((0, 256),)),
        "tangent_down": gaussian(keys[5], (FF, D), 1.0, 5.0, ((0, 256),)),
        "moment_up": gaussian(keys[6], (FF, D), 0.01, 0.15625, ((0, 256),)),
        "moment_down": gaussian(keys[7], (FF, D), 0.01, 0.15625, ((0, 256),)),
        "curve_up": jnp.clip(jnp.exp(math.log(4.0) - 2.9996462 * jax.random.uniform(keys[8], (FF, D), jnp.float32) ** levels(keys[8], (FF, D), ((0, 256),), -0.2, 0.2)), 0.19921875, 4.0).astype(jnp.bfloat16),
        "curve_down": jnp.clip(jnp.exp(math.log(4.0) - 2.9996462 * jax.random.uniform(keys[9], (FF, D), jnp.float32) ** levels(keys[9], (FF, D), ((0, 256),), -0.2, 0.2)), 0.19921875, 4.0).astype(jnp.bfloat16),
    }


beta_first = 0.965
beta_second = 0.99
gamma_scale = 0.01
ratio_floor = 0.01
root_half = 0.7071067811865476
inv_root_tau = 0.3989422804014327

def gelu_parts(pre_act):
    normal_cdf = 0.5 * (1.0 + lax.erf(pre_act * root_half))
    density = jnp.exp(-0.5 * pre_act * pre_act) * inv_root_tau
    return (pre_act * normal_cdf, normal_cdf + pre_act * density, density * (2.0 - pre_act * pre_act))

def times_transposed(left, right):
    return lax.dot_general(left, right, (((1,), (1,)), ((), ())), preferred_element_type=jnp.float32)

def transposed_times(left, right):
    return lax.dot_general(left, right, (((0,), (0,)), ((), ())), preferred_element_type=jnp.float32)

def refresh(moment, curve, grad, hvp, tangent):
    moment_f = beta_first * moment.astype(jnp.float32) + (1.0 - beta_first) * grad
    curve_f = beta_second * curve.astype(jnp.float32) + (1.0 - beta_second) * tangent.astype(jnp.float32) * hvp
    step = jnp.clip(moment_f / jnp.maximum(gamma_scale * curve_f, ratio_floor), -1.0, 1.0)
    return (step, moment_f.astype(jnp.bfloat16), curve_f.astype(jnp.bfloat16))

def reference(tokens, target, master_up, master_down, tangent_up, tangent_down, moment_up, moment_down, curve_up, curve_down):
    loss_scale = 1.0 / math.sqrt(TOKENS)
    weight_up = master_up.astype(jnp.bfloat16)
    weight_down = master_down.astype(jnp.bfloat16)
    pre_act = times_transposed(tokens, weight_up)
    pre_tangent = times_transposed(tokens, tangent_up)
    activated, slopes, bending = gelu_parts(pre_act)
    hidden = activated.astype(jnp.bfloat16)
    hidden_dot = (slopes * pre_tangent).astype(jnp.bfloat16)
    primal = jnp.dot(hidden, weight_down, preferred_element_type=jnp.float32)
    moved = jnp.dot(hidden_dot, weight_down, preferred_element_type=jnp.float32) + jnp.dot(hidden, tangent_down, preferred_element_type=jnp.float32)
    residual = (primal - target.astype(jnp.float32)).astype(jnp.bfloat16)
    residual_dot = moved.astype(jnp.bfloat16)
    back_grad = times_transposed(residual, weight_down)
    back_dot = times_transposed(residual_dot, weight_down) + times_transposed(residual, tangent_down)
    grad_pre = (back_grad * slopes).astype(jnp.bfloat16)
    grad_pre_dot = (back_dot * slopes + back_grad * bending * pre_tangent).astype(jnp.bfloat16)
    grad_up = loss_scale * transposed_times(grad_pre, tokens)
    hvp_up = loss_scale * transposed_times(grad_pre_dot, tokens)
    grad_down = loss_scale * transposed_times(hidden, residual)
    hvp_down = loss_scale * (transposed_times(hidden_dot, residual) + transposed_times(hidden, residual_dot))
    step_up, moment_up_next, curve_up_next = refresh(moment_up, curve_up, grad_up, hvp_up, tangent_up)
    step_down, moment_down_next, curve_down_next = refresh(moment_down, curve_down, grad_down, hvp_down, tangent_down)
    return (step_up, step_down, moment_up_next, moment_down_next, curve_up_next, curve_down_next)
```

```python
import math

import jax
import jax.numpy as jnp
from jax import lax
from jax.experimental import pallas as pl
from jax.experimental.pallas import tpu as pltpu
from jax.sharding import PartitionSpec as P

TOKENS = 512
D = 3072
HID = 96
PAD = 128
PARTS = 3
SIZE = {"y": 4, "x": 4, "z": 8}
AXES = ("y", "x", "z")
GATHER_ORDER = (("y", "z", "x"), ("z", "x", "y"), ("x", "y", "z"))
PART_ORDER = (2, 0, 1)
GROUP = 8
WIDE = D // GROUP
BLOCK = WIDE // PARTS

beta_first = 0.965
beta_second = 0.99
gamma_scale = 0.01
ratio_floor = 0.01
root_half = 0.7071067811865476
inv_root_tau = 0.3989422804014327

F32 = jnp.float32
BF16 = jnp.bfloat16
MESH = pl.DeviceIdType.MESH


def gelu_parts(pre_act):
    normal_cdf = 0.5 * (1.0 + lax.erf(pre_act * root_half))
    density = jnp.exp(-0.5 * pre_act * pre_act) * inv_root_tau
    return (
        pre_act * normal_cdf,
        normal_cdf + pre_act * density,
        density * (2.0 - pre_act * pre_act),
    )


def refresh(moment, curve, grad, hvp, tangent):
    moment_f = beta_first * moment.astype(F32) + (1.0 - beta_first) * grad
    curve_f = beta_second * curve.astype(F32) + (1.0 - beta_second) * tangent.astype(F32) * hvp
    step = jnp.clip(moment_f / jnp.maximum(gamma_scale * curve_f, ratio_floor), -1.0, 1.0)
    return step, moment_f.astype(BF16), curve_f.astype(BF16)


def wrap(value, size):
    return lax.rem(value + size, size)


def device(pos):
    y = pos["y"]
    return (
        lax.rem(y, 2) * 32 + pos["x"] * 8 + pos["z"],
        lax.div(y, 2) * 2 + pos["c"],
    )


def beside(pos, axis, by):
    return device({**pos, axis: wrap(pos[axis] + by, SIZE[axis])})


def place(where):
    return tuple(where[axis] for axis in AXES)


def halved(where, fulls, which):
    axis = fulls[0]
    half = SIZE[axis] // 2
    return {**where, axis: pl.ds(which * half, half)}


def gather_messages():
    table, count = {}, 0
    for part in range(PARTS):
        for phase, axis in enumerate(GATHER_ORDER[part]):
            for hop in range(SIZE[axis] // 2):
                for side in (1, -1):
                    table[(part, phase, hop, side)] = count
                    count += 1
        for number in range(SIZE[GATHER_ORDER[part][2]]):
            table[(part, number)] = count
            count += 1
    return table, count


GATHER_TABLE, GATHER_COUNT = gather_messages()


def scatter_messages():
    table, count = {}, 0
    for part in range(PARTS):
        for phase, axis in enumerate(GATHER_ORDER[part][::-1]):
            for hop in range(SIZE[axis] // 2):
                for side in (1, -1):
                    table[(part, phase, hop, side)] = count
                    count += 1
    return table, count


SCATTER_TABLE, SCATTER_COUNT = scatter_messages()


def gather_part(part, buffer, pos, send_sems, recv_sems, sent):
    mine = buffer.at[part, pos["c"]]
    other = buffer.at[part, 1 - pos["c"]]
    sibling = device({**pos, "c": 1 - pos["c"]})

    def copy(index, ref, target):
        return pltpu.make_async_remote_copy(
            src_ref=ref,
            dst_ref=ref,
            send_sem=send_sems.at[index],
            recv_sem=recv_sems.at[index],
            device_id=target,
            device_id_type=MESH,
        )

    def start(index, ref, target):
        made = copy(index, ref, target)
        made.start()
        sent.append(made)

    fulls = []
    arrivals = []
    for phase, axis in enumerate(GATHER_ORDER[part]):
        size = SIZE[axis]
        half = size // 2
        at = pos[axis]

        def chunk(offset, side=None):
            where = {**pos, axis: wrap(at + offset, size)}
            for full in fulls:
                where[full] = slice(None)
            if side is not None:
                where = halved(where, fulls, 0 if side == 1 else 1)
            return place(where)

        def moving(hop, side, behind):
            last = hop == half - 1
            if last and not fulls and side == -1:
                return None
            split = side if last and fulls else None
            return chunk(-side * (hop + behind), split)

        def await_hop(hop):
            for side in (1, -1):
                where = moving(hop, side, 1)
                if where is not None:
                    index = GATHER_TABLE[(part, phase, hop, side)]
                    copy(index, mine.at[where], sibling).wait_recv()

        def hand_on(offset, number):
            where = chunk(offset)
            index = GATHER_TABLE[(part, number)]
            start(index, mine.at[where], sibling)
            arrivals.append((index, where))

        for hop in range(half):
            if hop > 0:
                await_hop(hop - 1)
            for side in (1, -1):
                where = moving(hop, side, 0)
                if where is not None:
                    index = GATHER_TABLE[(part, phase, hop, side)]
                    start(index, mine.at[where], beside(pos, axis, side))
            if phase == 2:
                hand_on(-hop, 2 * hop)
                if hop > 0:
                    hand_on(hop, 2 * hop - 1)
            yield
        await_hop(half - 1)
        if phase == 2:
            hand_on(half, size - 1)
        fulls = [name for name in AXES if name in fulls or name == axis]
    yield
    for index, where in arrivals:
        copy(index, other.at[where], sibling).wait_recv()


def scatter_part(part, sums, boxes, pos, send_sems, recv_sems, sent):
    mine = sums.at[part]
    order = GATHER_ORDER[part][::-1]
    fulls = [name for name in AXES]
    for phase, axis in enumerate(order):
        size = SIZE[axis]
        half = size // 2
        at = pos[axis]
        box = boxes[part * 3 + phase]
        fulls = [name for name in fulls if name != axis]

        def chunk(offset, side=None):
            where = {**pos, axis: wrap(at + offset, size)}
            for full in fulls:
                where[full] = slice(None)
            if side is not None:
                where = halved(where, fulls, 0 if side == 1 else 1)
            return place(where)

        def slot(hop, side, split):
            where = {name: slice(None) for name in fulls}
            if split:
                where = halved(where, fulls, 0 if side == 1 else 1)
            lead = (0 if side == 1 else 1, hop)
            return lead + tuple(where[name] for name in AXES if name in fulls)

        def describe(hop, side):
            last = hop == half - 1
            if last and not fulls and side == -1:
                return None
            split = last and bool(fulls)
            return split, slot(hop, side, split)

        def copy(hop, side, source, into):
            index = SCATTER_TABLE[(part, phase, hop, side)]
            return pltpu.make_async_remote_copy(
                src_ref=mine.at[source],
                dst_ref=box.at[into],
                send_sem=send_sems.at[index],
                recv_sem=recv_sems.at[index],
                device_id=beside(pos, axis, side),
                device_id_type=MESH,
            )

        for hop in range(half - 1, -1, -1):
            for side in (1, -1):
                if hop < half - 1:
                    came = describe(hop + 1, side)
                    if came is not None:
                        split, into = came
                        where = chunk(side * (hop + 1), side if split else None)
                        copy(hop + 1, side, where, into).wait_recv()
                        mine[where] = (mine[where].astype(F32) + box[into].astype(F32)).astype(BF16)
                goes = describe(hop, side)
                if goes is not None:
                    split, into = goes
                    where = chunk(side * (hop + 1), side if split else None)
                    made = copy(hop, side, where, into)
                    made.start()
                    sent.append(made)
            yield
        where = chunk(0)
        total = mine[where].astype(F32)
        for side in (1, -1):
            split, into = describe(0, side)
            copy(0, side, where, into).wait_recv()
            total = total + box[into].astype(F32)
        if phase < 2:
            mine[where] = total.astype(BF16)
        else:
            yield total
            return


def together(runs):
    alive = dict(runs)
    result = {}
    while alive:
        for part in list(alive):
            try:
                result[part] = next(alive[part])
            except StopIteration:
                del alive[part]
    return result


def kernel(
    tokens,
    target,
    master_up,
    master_down,
    tangent_up,
    tangent_down,
    moment_up,
    moment_down,
    curve_up,
    curve_down,
    step_up,
    step_down,
    moment_up_next,
    moment_down_next,
    curve_up_next,
    curve_down_next,
    v_master_up,
    v_master_down,
    v_tangent_up,
    v_tangent_down,
    v_moment_up,
    v_moment_down,
    v_curve_up,
    v_curve_down,
    o_step_up,
    o_step_down,
    o_moment_up,
    o_moment_down,
    o_curve_up,
    o_curve_down,
    group,
    goal,
    all_tokens,
    weights_up,
    weights_down,
    acc,
    both,
    both_t,
    grads_t,
    slopes_ref,
    bend_ref,
    outgoing,
    incoming,
    sums,
    residuals,
    *rest,
):
    boxes = rest[: 3 * PARTS]
    in_sems, out_sems, pair_send, pair_recv, group_send, group_recv = rest[9:15]
    first_send, first_recv, scatter_send, scatter_recv, second_send, second_recv = rest[15:]

    dp = lax.axis_index("dp")
    tensor = lax.axis_index("tensor")
    core = lax.rem(tensor, 2)
    pos = {
        "x": lax.rem(lax.div(dp, 8), 4),
        "z": lax.rem(dp, 8),
        "y": lax.div(tensor, 2) * 2 + lax.div(dp, 32),
        "c": core,
    }
    me = core * 4 + pos["y"]
    sent = []

    loads = []
    pairs = (
        (master_up, v_master_up),
        (tangent_up, v_tangent_up),
        (master_down, v_master_down),
        (tangent_down, v_tangent_down),
        (moment_up, v_moment_up),
        (moment_down, v_moment_down),
        (curve_up, v_curve_up),
        (curve_down, v_curve_down),
    )
    for number, (source, into) in enumerate(pairs):
        made = pltpu.make_async_copy(source, into, in_sems.at[number])
        made.start()
        loads.append(made)

    def member(by):
        spot = lax.rem(me + by, GROUP)
        return device({**pos, "c": lax.div(spot, 4), "y": lax.rem(spot, 4)})

    barrier = pltpu.get_barrier_semaphore()
    peers = [member(by) for by in range(1, GROUP)]
    peers += [beside(pos, axis, side) for axis in ("x", "z") for side in (1, -1)]
    for peer in peers:
        pl.semaphore_signal(barrier, inc=1, device_id=peer, device_id_type=MESH)

    rows = jnp.concatenate([tokens[...].astype(F32), target[...].astype(F32)], axis=0)
    pieces = []
    for lead in (0, 2):
        pieces.append(
            jnp.concatenate(
                [rows[lead : lead + 2, k * WIDE : (k + 1) * WIDE] for k in range(GROUP)], axis=0
            )
        )
    group[me] = jnp.concatenate(pieces, axis=1).astype(BF16)
    pl.semaphore_wait(barrier, len(peers))

    def group_copy(by, spot):
        return pltpu.make_async_remote_copy(
            src_ref=group.at[spot],
            dst_ref=group.at[spot],
            send_sem=group_send.at[by],
            recv_sem=group_recv.at[by],
            device_id=member(by),
            device_id_type=MESH,
        )

    for by in range(1, GROUP):
        made = group_copy(by, me)
        made.start()
        sent.append(made)

    for made in loads[:4]:
        made.wait()
    zeros_up = jnp.zeros((PAD - HID, 768), BF16)
    for k in range(4):
        columns = slice(k * 768, (k + 1) * 768)
        weights_up[k, 0:HID] = v_master_up[:, columns].astype(BF16)
        weights_up[k, HID:PAD] = zeros_up
        weights_up[k, PAD : PAD + HID] = v_tangent_up[:, columns]
        weights_up[k, PAD + HID :] = zeros_up
    zeros_low = jnp.zeros((PAD - HID, 2 * BLOCK), BF16)
    zeros_half = jnp.zeros((HID, BLOCK), BF16)
    for spot in range(GROUP):
        for part in range(PARTS):
            start = spot * WIDE + part * BLOCK
            columns = slice(start, start + BLOCK)
            into = weights_down.at[part, spot // 4, spot % 4]
            weight = v_master_down[:, columns].astype(BF16)
            into[0:HID, 0:BLOCK] = weight
            into[0:HID, BLOCK:] = v_tangent_down[:, columns]
            into[HID:PAD] = zeros_low
            into[PAD : PAD + HID, 0:BLOCK] = zeros_half
            into[PAD : PAD + HID, BLOCK:] = weight
            into[PAD + HID :] = zeros_low

    for by in range(1, GROUP):
        group_copy(by, lax.rem(me + GROUP - by, GROUP)).wait_recv()
    row = lax.broadcasted_iota(jnp.int32, (16, 128), 0)
    column = lax.broadcasted_iota(jnp.int32, (16, 128), 1)
    pick = (column == lax.div(row, 2) * 16 + me * 2 + lax.rem(row, 2)).astype(F32).astype(BF16)
    picked = jnp.dot(pick, group[...].reshape(128, 2 * WIDE), preferred_element_type=F32)
    goal[...] = picked[:, WIDE:]
    for part in range(PARTS):
        own = all_tokens.at[part, core, pos["y"], pos["x"], pos["z"]]
        own[...] = picked[:, part * BLOCK : (part + 1) * BLOCK].astype(BF16)

    together(
        (part, gather_part(part, all_tokens, pos, first_send, first_recv, sent))
        for part in PART_ORDER
    )

    acc[...] = jnp.zeros_like(acc)

    @pl.loop(0, 4)
    def _(k):
        spot = 2 * k
        blocks = []
        for lower in range(2):
            for part in range(PARTS):
                block = all_tokens[part, lax.div(spot, 4), lax.rem(spot, 4) + lower]
                blocks.append(block.reshape(TOKENS, BLOCK))
        acc[...] += lax.dot_general(
            jnp.concatenate(blocks, axis=1),
            weights_up[k],
            (((1,), (1,)), ((), ())),
            preferred_element_type=F32,
        )

    @pl.loop(0, 4)
    def _(k):
        span = pl.ds(pl.multiple_of(k * 128, 128), 128)
        pre_tangent = acc[span, PAD:]
        activated, slopes, bending = gelu_parts(acc[span, :PAD])
        slopes_ref[span] = slopes
        bend_ref[span] = bending * pre_tangent
        pair = jnp.concatenate([activated, slopes * pre_tangent], axis=1)
        both[span] = pair.astype(BF16)

    sibling = device({**pos, "c": 1 - core})

    def pair_copy(part):
        return pltpu.make_async_remote_copy(
            src_ref=outgoing.at[part],
            dst_ref=incoming.at[part],
            send_sem=pair_send.at[part],
            recv_sem=pair_recv.at[part],
            device_id=sibling,
            device_id_type=MESH,
        )

    for part in PART_ORDER:

        @pl.loop(0, 4)
        def _(y):
            block = jnp.dot(
                both[...], weights_down[part, 1 - core, y], preferred_element_type=F32
            )
            outgoing[part, y] = block.astype(BF16).reshape(4, 8, 16, 2 * BLOCK)

        made = pair_copy(part)
        made.start()
        sent.append(made)

    scatters = {}
    for part in PART_ORDER:
        pair_copy(part).wait_recv()

        @pl.loop(0, 4)
        def _(y):
            block = jnp.dot(both[...], weights_down[part, core, y], preferred_element_type=F32)
            block = block + incoming[part, y].astype(F32).reshape(TOKENS, 2 * BLOCK)
            sums[part, y] = block.astype(BF16).reshape(4, 8, 16, 2 * BLOCK)

        scatters[part] = scatter_part(part, sums, boxes, pos, scatter_send, scatter_recv, sent)
        next(scatters[part])

    both_t[...] = both[...].astype(F32).T.astype(BF16)
    totals = together(scatters.items())
    for part in PART_ORDER:
        total = totals[part]
        residual = total[:, :BLOCK] - goal[:, part * BLOCK : (part + 1) * BLOCK]
        own = residuals.at[part, core, pos["y"], pos["x"], pos["z"]]
        own[...] = jnp.concatenate([total[:, BLOCK:], residual], axis=1).astype(BF16)

    together(
        (part, gather_part(part, residuals, pos, second_send, second_recv, sent))
        for part in PART_ORDER
    )

    acc[...] = jnp.zeros_like(acc)

    @pl.loop(0, GROUP)
    def _(spot):
        half, y = lax.div(spot, 4), lax.rem(spot, 4)
        left = [residuals[part, half, y].reshape(TOKENS, 2 * BLOCK) for part in range(PARTS)]
        right = [weights_down[part, half, y] for part in range(PARTS)]
        acc[...] += lax.dot_general(
            jnp.concatenate(left, axis=1),
            jnp.concatenate(right, axis=1),
            (((1,), (1,)), ((), ())),
            preferred_element_type=F32,
        )

    for k in range(4):
        span = slice(k * 128, (k + 1) * 128)
        back_dot, back_grad = acc[span, :PAD], acc[span, PAD:]
        slopes = slopes_ref[span]
        grad_pre = (back_grad * slopes).T.astype(BF16)
        grad_pre_dot = (back_dot * slopes + back_grad * bend_ref[span]).T.astype(BF16)
        grads_t[0:PAD, span] = grad_pre
        grads_t[PAD:, span] = grad_pre_dot

    for made in loads[4:]:
        made.wait()
    loss_scale = 1.0 / math.sqrt(TOKENS)
    results = (
        (o_step_up, step_up),
        (o_step_down, step_down),
        (o_moment_up, moment_up_next),
        (o_moment_down, moment_down_next),
        (o_curve_up, curve_up_next),
        (o_curve_down, curve_down_next),
    )

    def store(number, spot):
        source, into = results[number]
        span = pl.ds(pl.multiple_of(spot * WIDE, 128), WIDE)
        return pltpu.make_async_copy(
            source.at[:, span], into.at[:, span], out_sems.at[number, spot]
        )

    @pl.loop(0, GROUP)
    def _(spot):
        half, y = lax.div(spot, 4), lax.rem(spot, 4)
        span = pl.ds(pl.multiple_of(spot * WIDE, 128), WIDE)
        right = [all_tokens[part, half, y].reshape(TOKENS, BLOCK) for part in range(PARTS)]
        up = jnp.dot(
            grads_t[...], jnp.concatenate(right, axis=1), preferred_element_type=F32
        )
        o_step_up[:, span], o_moment_up[:, span], o_curve_up[:, span] = refresh(
            v_moment_up[:, span],
            v_curve_up[:, span],
            loss_scale * up[:HID],
            loss_scale * up[PAD : PAD + HID],
            v_tangent_up[:, span],
        )
        grad, hvp = [], []
        for part in range(PARTS):
            down = jnp.dot(
                both_t[...],
                residuals[part, half, y].reshape(TOKENS, 2 * BLOCK),
                preferred_element_type=F32,
            )
            grad.append(down[:HID, BLOCK:])
            hvp.append(down[:HID, :BLOCK] + down[PAD : PAD + HID, BLOCK:])
        o_step_down[:, span], o_moment_down[:, span], o_curve_down[:, span] = refresh(
            v_moment_down[:, span],
            v_curve_down[:, span],
            loss_scale * jnp.concatenate(grad, axis=1),
            loss_scale * jnp.concatenate(hvp, axis=1),
            v_tangent_down[:, span],
        )
        for number in range(6):
            store(number, spot).start()

    for made in sent:
        made.wait_send()

    @pl.loop(0, GROUP)
    def _(spot):
        for number in range(6):
            store(number, spot).wait()


def box_shapes():
    shapes = []
    for part in range(PARTS):
        fulls = list(AXES)
        for axis in GATHER_ORDER[part][::-1]:
            fulls.remove(axis)
            lead = (2, SIZE[axis] // 2) + tuple(SIZE[name] for name in fulls)
            shapes.append(pltpu.VMEM(lead + (16, 2 * BLOCK), BF16))
    return shapes


def per_device(*arrays):
    wide32 = jax.ShapeDtypeStruct((HID, D), F32)
    wide16 = jax.ShapeDtypeStruct((HID, D), BF16)
    blocks = (4, 4, 8, 16)
    any_spec = pl.BlockSpec(memory_space=pl.ANY)
    scratch = [pltpu.VMEM((HID, D), F32)] * 2 + [pltpu.VMEM((HID, D), BF16)] * 6
    scratch += [pltpu.VMEM((HID, D), F32)] * 2 + [pltpu.VMEM((HID, D), BF16)] * 4
    scratch += [
        pltpu.VMEM((GROUP, 16, 2 * WIDE), BF16),
        pltpu.VMEM((16, WIDE), F32),
        pltpu.VMEM((PARTS, 2) + blocks + (BLOCK,), BF16),
        pltpu.VMEM((4, 2 * PAD, 768), BF16),
        pltpu.VMEM((PARTS, 2, 4, 2 * PAD, 2 * BLOCK), BF16),
        pltpu.VMEM((TOKENS, 2 * PAD), F32),
        pltpu.VMEM((TOKENS, 2 * PAD), BF16),
        pltpu.VMEM((2 * PAD, TOKENS), BF16),
        pltpu.VMEM((2 * PAD, TOKENS), BF16),
        pltpu.VMEM((TOKENS, PAD), F32),
        pltpu.VMEM((TOKENS, PAD), F32),
        pltpu.VMEM((PARTS,) + blocks + (2 * BLOCK,), BF16),
        pltpu.VMEM((PARTS,) + blocks + (2 * BLOCK,), BF16),
        pltpu.VMEM((PARTS,) + blocks + (2 * BLOCK,), BF16),
        pltpu.VMEM((PARTS, 2) + blocks + (2 * BLOCK,), BF16),
    ]
    scratch += box_shapes()
    dma = pltpu.SemaphoreType.DMA
    scratch += [
        dma((8,)),
        dma((6, GROUP)),
        dma((PARTS,)),
        dma((PARTS,)),
        dma((GROUP,)),
        dma((GROUP,)),
        dma((GATHER_COUNT,)),
        dma((GATHER_COUNT,)),
        dma((SCATTER_COUNT,)),
        dma((SCATTER_COUNT,)),
        dma((GATHER_COUNT,)),
        dma((GATHER_COUNT,)),
    ]
    return pl.pallas_call(
        kernel,
        out_shape=(wide32, wide32, wide16, wide16, wide16, wide16),
        in_specs=[pl.BlockSpec(memory_space=pltpu.VMEM)] * 2 + [any_spec] * 8,
        out_specs=(any_spec,) * 6,
        scratch_shapes=scratch,
        compiler_params=pltpu.CompilerParams(
            collective_id=0, has_side_effects=True, vmem_limit_bytes=60 * 1024 * 1024
        ),
        cost_estimate=pl.CostEstimate(
            flops=4_000_000_000, bytes_accessed=11_000_000, transcendentals=131072
        ),
    )(*arrays)


def solution(mesh):
    rows = P(("dp", "tensor"), None)
    return jax.shard_map(
        per_device, mesh=mesh, in_specs=(rows,) * 10, out_specs=(rows,) * 6, check_vma=False
    )
```

```python
import math

import jax
import jax.numpy as jnp
from jax import lax
from jax.experimental import pallas as pl
from jax.experimental.pallas import tpu as pltpu
from jax.sharding import PartitionSpec as P

TOKENS = 512
D = 3072
HID = 96
PAD = 128
PARTS = 3
SIZE = {"y": 4, "x": 4, "z": 8}
AXES = ("y", "x", "z")
GROUP = 8
WIDE = D // GROUP
NEAR = (2, 1, 3)
LONG = (4, 3, 5, 2, 6, 1, 7)
PARTS = (("y", "x"), ("x", "y"))
GATHER_COUNT = 7 + 2 * 15 + 2 * 16
SCATTER_COUNT = 2 * (12 + 3) + 7

beta_first = 0.965
beta_second = 0.99
gamma_scale = 0.01
ratio_floor = 0.01
root_half = 0.7071067811865476
inv_root_tau = 0.3989422804014327

F32 = jnp.float32
BF16 = jnp.bfloat16
MESH = pl.DeviceIdType.MESH


def gelu_parts(pre_act):
    normal_cdf = 0.5 * (1.0 + lax.erf(pre_act * root_half))
    density = jnp.exp(-0.5 * pre_act * pre_act) * inv_root_tau
    return (
        pre_act * normal_cdf,
        normal_cdf + pre_act * density,
        density * (2.0 - pre_act * pre_act),
    )


def refresh(moment, curve, grad, hvp, tangent):
    moment_f = beta_first * moment.astype(F32) + (1.0 - beta_first) * grad
    curve_f = beta_second * curve.astype(F32) + (1.0 - beta_second) * tangent.astype(F32) * hvp
    step = jnp.clip(moment_f / jnp.maximum(gamma_scale * curve_f, ratio_floor), -1.0, 1.0)
    return step, moment_f.astype(BF16), curve_f.astype(BF16)


def wrap(value, size):
    return lax.rem(value + size, size)


def device(pos):
    y = pos["y"]
    return (
        lax.rem(y, 2) * 32 + pos["x"] * 8 + pos["z"],
        lax.div(y, 2) * 2 + pos["c"],
    )


def beside(pos, axis, by):
    return device({**pos, axis: wrap(pos[axis] + by, SIZE[axis])})


def place(where):
    return tuple(where[axis] for axis in AXES)


def half_rows(part):
    return pl.ds(part * 4, 4)


def gather(buffer, pos, send_sems, recv_sems, sent):
    mine = buffer.at[pos["c"]]
    other = buffer.at[1 - pos["c"]]
    sibling = device({**pos, "c": 1 - pos["c"]})

    def copy(index, ref, target):
        return pltpu.make_async_remote_copy(
            src_ref=ref,
            dst_ref=ref,
            send_sem=send_sems.at[index],
            recv_sem=recv_sems.at[index],
            device_id=target,
            device_id_type=MESH,
        )

    def start(index, ref, target):
        made = copy(index, ref, target)
        made.start()
        sent.append(made)

    def block(part, back_middle, back_final):
        middle, final = PARTS[part]
        where = {
            middle: wrap(pos[middle] - back_middle, 4),
            final: wrap(pos[final] - back_final, 4),
            "z": half_rows(part),
        }
        return place(where)

    def hand_on(part, m, f):
        start(37 + part * 16 + m * 4 + f, mine.at[block(part, m, f)], sibling)

    own = mine.at[place(pos)]
    for by in LONG:
        start(by - 1, own, beside(pos, "z", by))
    yield
    for by in LONG[::-1]:
        came = mine.at[place({**pos, "z": wrap(pos["z"] - by, 8)})]
        copy(by - 1, came, sibling).wait_recv()
    for part in range(2):
        for m in NEAR:
            start(7 + part * 15 + m - 1, mine.at[block(part, 0, 0)], beside(pos, PARTS[part][0], m))
    for part in range(2):
        for f in NEAR:
            start(10 + part * 15 + f - 1, mine.at[block(part, 0, 0)], beside(pos, PARTS[part][1], f))
        hand_on(part, 0, 0)
    for m in (1, 3, 2):
        for part in range(2):
            came = mine.at[block(part, m, 0)]
            copy(7 + part * 15 + m - 1, came, sibling).wait_recv()
            for f in NEAR:
                index = 13 + part * 15 + (m - 1) * 3 + f - 1
                start(index, came, beside(pos, PARTS[part][1], f))
            hand_on(part, m, 0)
    for m in (0, 1, 3, 2):
        for f in (1, 3, 2):
            for part in range(2):
                index = (10 if m == 0 else 13 + (m - 1) * 3) + part * 15 + f - 1
                copy(index, mine.at[block(part, m, f)], sibling).wait_recv()
                hand_on(part, m, f)
    for m in (0, 1, 3, 2):
        for f in (0, 1, 3, 2):
            for part in range(2):
                index = 37 + part * 16 + m * 4 + f
                copy(index, other.at[block(part, m, f)], sibling).wait_recv()


class Scatter:
    def __init__(self, sums, boxes, pos, send_sems, recv_sems, sent):
        self.sums, self.boxes, self.pos = sums, boxes, pos
        self.send_sems, self.recv_sems, self.sent = send_sems, recv_sems, sent

    def copy(self, index, source, into, target):
        return pltpu.make_async_remote_copy(
            src_ref=source,
            dst_ref=into,
            send_sem=self.send_sems.at[index],
            recv_sem=self.recv_sems.at[index],
            device_id=target,
            device_id_type=MESH,
        )

    def start(self, *what):
        made = self.copy(*what)
        made.start()
        self.sent.append(made)

    def piece(self, part, by_first, by_second):
        second, first = PARTS[part]
        where = {
            first: wrap(self.pos[first] + by_first, 4),
            second: wrap(self.pos[second] + by_second, 4),
            "z": half_rows(part),
        }
        return place(where)

    def first(self, part, by_first, by_second):
        index = part * 15 + (by_first - 1) * 4 + by_second
        self.start(
            index,
            self.sums.at[self.piece(part, by_first, by_second)],
            self.boxes[0].at[part, by_first - 1, by_second],
            beside(self.pos, PARTS[part][1], by_first),
        )

    def second(self, part, by_second):
        box = self.boxes[0]
        where = self.piece(part, 0, by_second)
        total = self.sums[where].astype(F32)
        for by in (1, 3, 2):
            index = part * 15 + (by - 1) * 4 + by_second
            into = box.at[part, by - 1, by_second]
            self.copy(index, self.sums.at[where], into, beside(self.pos, "x", 1)).wait_recv()
            total = total + box[part, by - 1, by_second].astype(F32)
        if by_second:
            self.sums[where] = total.astype(BF16)
            self.start(
                part * 15 + 12 + by_second - 1,
                self.sums.at[where],
                self.boxes[1].at[part, by_second - 1],
                beside(self.pos, PARTS[part][0], by_second),
            )
            return
        for by in (1, 3, 2):
            into = self.boxes[1].at[part, by - 1]
            index = part * 15 + 12 + by - 1
            self.copy(index, self.sums.at[where], into, beside(self.pos, "x", 1)).wait_recv()
            total = total + self.boxes[1][part, by - 1].astype(F32)
        self.sums[where] = total.astype(BF16)

    def third(self):
        for by in LONG:
            self.start(
                30 + by - 1,
                self.sums.at[place({**self.pos, "z": wrap(self.pos["z"] + by, 8)})],
                self.boxes[2].at[by - 1],
                beside(self.pos, "z", by),
            )
        where = place(self.pos)
        total = self.sums[where].astype(F32)
        for by in LONG[::-1]:
            into = self.boxes[2].at[by - 1]
            self.copy(30 + by - 1, self.sums.at[where], into, beside(self.pos, "x", 1)).wait_recv()
            total = total + self.boxes[2][by - 1].astype(F32)
        return total


def kernel(
    tokens,
    target,
    master_up,
    master_down,
    tangent_up,
    tangent_down,
    moment_up,
    moment_down,
    curve_up,
    curve_down,
    step_up,
    step_down,
    moment_up_next,
    moment_down_next,
    curve_up_next,
    curve_down_next,
    v_master_up,
    v_master_down,
    v_tangent_up,
    v_tangent_down,
    v_moment_up,
    v_moment_down,
    v_curve_up,
    v_curve_down,
    o_step_up,
    o_step_down,
    o_moment_up,
    o_moment_down,
    o_curve_up,
    o_curve_down,
    group,
    folded,
    all_tokens,
    weights_up,
    weights_down,
    acc,
    both,
    both_t,
    grads_t,
    slopes_ref,
    bend_ref,
    outgoing,
    incoming,
    sums,
    residuals,
    *rest,
):
    boxes = rest[:3]
    in_sems, out_sems, pair_send, pair_recv, group_send, group_recv = rest[3:9]
    first_send, first_recv, scatter_send, scatter_recv, second_send, second_recv = rest[9:]

    dp = lax.axis_index("dp")
    tensor = lax.axis_index("tensor")
    core = lax.rem(tensor, 2)
    pos = {
        "x": lax.rem(lax.div(dp, 8), 4),
        "z": lax.rem(dp, 8),
        "y": lax.div(tensor, 2) * 2 + lax.div(dp, 32),
        "c": core,
    }
    me = core * 4 + pos["y"]
    sent = []

    loads = []
    pairs = (
        (master_up, v_master_up),
        (tangent_up, v_tangent_up),
        (master_down, v_master_down),
        (tangent_down, v_tangent_down),
        (moment_up, v_moment_up),
        (moment_down, v_moment_down),
        (curve_up, v_curve_up),
        (curve_down, v_curve_down),
    )
    for number, (source, into) in enumerate(pairs):
        made = pltpu.make_async_copy(source, into, in_sems.at[number])
        made.start()
        loads.append(made)

    def member(by):
        spot = lax.rem(me + by, GROUP)
        return device({**pos, "c": lax.div(spot, 4), "y": lax.rem(spot, 4)})

    barrier = pltpu.get_barrier_semaphore()
    peers = [member(by) for by in range(1, GROUP)]
    peers += [beside(pos, "x", by) for by in range(1, 4)]
    peers += [beside(pos, "z", by) for by in range(1, 8)]
    for peer in peers:
        pl.semaphore_signal(barrier, inc=1, device_id=peer, device_id_type=MESH)

    def fold(rows):
        rows = rows.astype(F32)
        pieces = [rows[:, k * WIDE : (k + 1) * WIDE] for k in range(GROUP)]
        return jnp.concatenate(pieces, axis=0).astype(BF16)

    folded[core, pos["y"], pos["x"], pos["z"]] = fold(tokens[...])
    group[me] = fold(target[...])

    loads[0].wait()
    loads[1].wait()
    zeros_up = jnp.zeros((PAD - HID, 768), BF16)
    for k in range(4):
        columns = slice(k * 768, (k + 1) * 768)
        weights_up[k, 0:HID] = v_master_up[:, columns].astype(BF16)
        weights_up[k, HID:PAD] = zeros_up
        weights_up[k, PAD : PAD + HID] = v_tangent_up[:, columns]
        weights_up[k, PAD + HID :] = zeros_up
    pl.semaphore_wait(barrier, len(peers))

    first = gather(folded, pos, first_send, first_recv, sent)
    next(first)

    def group_copy(by, spot):
        return pltpu.make_async_remote_copy(
            src_ref=group.at[spot],
            dst_ref=group.at[spot],
            send_sem=group_send.at[by],
            recv_sem=group_recv.at[by],
            device_id=member(by),
            device_id_type=MESH,
        )

    for by in range(1, GROUP):
        made = group_copy(by, me)
        made.start()
        sent.append(made)

    loads[2].wait()
    loads[3].wait()
    zeros_low = jnp.zeros((PAD - HID, 2 * WIDE), BF16)
    zeros_half = jnp.zeros((HID, WIDE), BF16)
    for spot in range(GROUP):
        columns = slice(spot * WIDE, (spot + 1) * WIDE)
        weight = v_master_down[:, columns].astype(BF16)
        weights_down[spot, 0:HID, 0:WIDE] = weight
        weights_down[spot, 0:HID, WIDE:] = v_tangent_down[:, columns]
        weights_down[spot, HID:PAD] = zeros_low
        weights_down[spot, PAD : PAD + HID, 0:WIDE] = zeros_half
        weights_down[spot, PAD : PAD + HID, WIDE:] = weight
        weights_down[spot, PAD + HID :] = zeros_low

    for _ in first:
        pass

    row = lax.broadcasted_iota(jnp.int32, (128, 128), 0)
    column = lax.broadcasted_iota(jnp.int32, (128, 128), 1)
    token = lax.rem(row, 16)
    pick = column == lax.div(token, 2) * 16 + lax.div(row, 16) * 2 + lax.rem(token, 2)
    pick = pick.astype(F32).astype(BF16)

    @pl.loop(0, 4)
    def _(x):
        for z in range(8):
            blocks = folded[:, :, x, z].reshape(128, WIDE)
            rows = jnp.dot(pick, blocks, preferred_element_type=F32).astype(BF16)
            all_tokens[:, x, z] = rows.reshape(GROUP, 16, WIDE)

    acc[...] = jnp.zeros_like(acc)

    @pl.loop(0, 4)
    def _(k):
        blocks = [all_tokens[2 * k + lower].reshape(TOKENS, WIDE) for lower in range(2)]
        acc[...] += lax.dot_general(
            jnp.concatenate(blocks, axis=1),
            weights_up[k],
            (((1,), (1,)), ((), ())),
            preferred_element_type=F32,
        )

    @pl.loop(0, 4)
    def _(k):
        span = pl.ds(pl.multiple_of(k * 128, 128), 128)
        pre_tangent = acc[span, PAD:]
        activated, slopes, bending = gelu_parts(acc[span, :PAD])
        slopes_ref[span] = slopes
        bend_ref[span] = bending * pre_tangent
        pair = jnp.concatenate([activated, slopes * pre_tangent], axis=1)
        both[span] = pair.astype(BF16)

    sibling = device({**pos, "c": 1 - core})

    def pair_copy(by):
        return pltpu.make_async_remote_copy(
            src_ref=outgoing.at[by],
            dst_ref=incoming.at[by],
            send_sem=pair_send.at[by],
            recv_sem=pair_recv.at[by],
            device_id=sibling,
            device_id_type=MESH,
        )

    turns = (1, 3, 2, 0)
    for by in turns:
        spot = (1 - core) * 4 + wrap(pos["y"] + by, 4)
        block = jnp.dot(both[...], weights_down[spot], preferred_element_type=F32)
        outgoing[by] = block.astype(BF16).reshape(4, 8, 16, 2 * WIDE)
        made = pair_copy(by)
        made.start()
        sent.append(made)

    scatter = Scatter(sums, boxes, pos, scatter_send, scatter_recv, sent)
    for by in turns:
        pair_copy(by).wait_recv()
        y = wrap(pos["y"] + by, 4)
        block = jnp.dot(both[...], weights_down[core * 4 + y], preferred_element_type=F32)
        block = block + incoming[by].astype(F32).reshape(TOKENS, 2 * WIDE)
        sums[y] = block.astype(BF16).reshape(4, 8, 16, 2 * WIDE)
        for to in NEAR:
            scatter.first(0, to, by)
        if by:
            for to in turns:
                scatter.first(1, by, to)

    both_t[...] = both[...].astype(F32).T.astype(BF16)
    for by in turns:
        for part in range(2):
            scatter.second(part, by)
    total = scatter.third()

    for by in range(1, GROUP):
        group_copy(by, lax.rem(me + GROUP - by, GROUP)).wait_recv()
    row = lax.broadcasted_iota(jnp.int32, (16, 128), 0)
    column = lax.broadcasted_iota(jnp.int32, (16, 128), 1)
    pick = (column == lax.div(row, 2) * 16 + me * 2 + lax.rem(row, 2)).astype(F32).astype(BF16)
    goal = jnp.dot(pick, group[...].reshape(128, WIDE), preferred_element_type=F32)
    pair = jnp.concatenate([total[:, WIDE:], total[:, :WIDE] - goal], axis=1)
    residuals[core, pos["y"], pos["x"], pos["z"]] = pair.astype(BF16)

    for _ in gather(residuals, pos, second_send, second_recv, sent):
        pass

    acc[...] = jnp.zeros_like(acc)

    @pl.loop(0, GROUP)
    def _(spot):
        acc[...] += lax.dot_general(
            residuals[lax.div(spot, 4), lax.rem(spot, 4)].reshape(TOKENS, 2 * WIDE),
            weights_down[spot],
            (((1,), (1,)), ((), ())),
            preferred_element_type=F32,
        )

    for k in range(4):
        span = slice(k * 128, (k + 1) * 128)
        back_dot, back_grad = acc[span, :PAD], acc[span, PAD:]
        slopes = slopes_ref[span]
        grad_pre = (back_grad * slopes).T.astype(BF16)
        grad_pre_dot = (back_dot * slopes + back_grad * bend_ref[span]).T.astype(BF16)
        grads_t[0:PAD, span] = grad_pre
        grads_t[PAD:, span] = grad_pre_dot

    for made in loads[4:]:
        made.wait()
    loss_scale = 1.0 / math.sqrt(TOKENS)
    results = (
        (o_step_up, step_up),
        (o_step_down, step_down),
        (o_moment_up, moment_up_next),
        (o_moment_down, moment_down_next),
        (o_curve_up, curve_up_next),
        (o_curve_down, curve_down_next),
    )

    def store(number, spot):
        source, into = results[number]
        span = pl.ds(pl.multiple_of(spot * WIDE, 128), WIDE)
        return pltpu.make_async_copy(
            source.at[:, span], into.at[:, span], out_sems.at[number, spot]
        )

    @pl.loop(0, GROUP)
    def _(spot):
        span = pl.ds(pl.multiple_of(spot * WIDE, 128), WIDE)
        up = jnp.dot(
            grads_t[...], all_tokens[spot].reshape(TOKENS, WIDE), preferred_element_type=F32
        )
        o_step_up[:, span], o_moment_up[:, span], o_curve_up[:, span] = refresh(
            v_moment_up[:, span],
            v_curve_up[:, span],
            loss_scale * up[:HID],
            loss_scale * up[PAD : PAD + HID],
            v_tangent_up[:, span],
        )
        down = jnp.dot(
            both_t[...],
            residuals[lax.div(spot, 4), lax.rem(spot, 4)].reshape(TOKENS, 2 * WIDE),
            preferred_element_type=F32,
        )
        o_step_down[:, span], o_moment_down[:, span], o_curve_down[:, span] = refresh(
            v_moment_down[:, span],
            v_curve_down[:, span],
            loss_scale * down[:HID, WIDE:],
            loss_scale * (down[:HID, :WIDE] + down[PAD : PAD + HID, WIDE:]),
            v_tangent_down[:, span],
        )
        for number in range(6):
            store(number, spot).start()

    for made in sent:
        made.wait_send()

    @pl.loop(0, GROUP)
    def _(spot):
        for number in range(6):
            store(number, spot).wait()


def per_device(*arrays):
    wide32 = jax.ShapeDtypeStruct((HID, D), F32)
    wide16 = jax.ShapeDtypeStruct((HID, D), BF16)
    blocks = (4, 4, 8, 16)
    any_spec = pl.BlockSpec(memory_space=pl.ANY)
    scratch = [pltpu.VMEM((HID, D), F32)] * 2 + [pltpu.VMEM((HID, D), BF16)] * 6
    scratch += [pltpu.VMEM((HID, D), F32)] * 2 + [pltpu.VMEM((HID, D), BF16)] * 4
    scratch += [
        pltpu.VMEM((GROUP, 16, WIDE), BF16),
        pltpu.VMEM((2,) + blocks + (WIDE,), BF16),
        pltpu.VMEM((GROUP, 4, 8, 16, WIDE), BF16),
        pltpu.VMEM((4, 2 * PAD, 768), BF16),
        pltpu.VMEM((GROUP, 2 * PAD, 2 * WIDE), BF16),
        pltpu.VMEM((TOKENS, 2 * PAD), F32),
        pltpu.VMEM((TOKENS, 2 * PAD), BF16),
        pltpu.VMEM((2 * PAD, TOKENS), BF16),
        pltpu.VMEM((2 * PAD, TOKENS), BF16),
        pltpu.VMEM((TOKENS, PAD), F32),
        pltpu.VMEM((TOKENS, PAD), F32),
        pltpu.VMEM(blocks + (2 * WIDE,), BF16),
        pltpu.VMEM(blocks + (2 * WIDE,), BF16),
        pltpu.VMEM(blocks + (2 * WIDE,), BF16),
        pltpu.VMEM((2,) + blocks + (2 * WIDE,), BF16),
        pltpu.VMEM((2, 3, 4, 4, 16, 2 * WIDE), BF16),
        pltpu.VMEM((2, 3, 4, 16, 2 * WIDE), BF16),
        pltpu.VMEM((7, 16, 2 * WIDE), BF16),
    ]
    dma = pltpu.SemaphoreType.DMA
    scratch += [
        dma((8,)),
        dma((6, GROUP)),
        dma((4,)),
        dma((4,)),
        dma((GROUP,)),
        dma((GROUP,)),
        dma((GATHER_COUNT,)),
        dma((GATHER_COUNT,)),
        dma((SCATTER_COUNT,)),
        dma((SCATTER_COUNT,)),
        dma((GATHER_COUNT,)),
        dma((GATHER_COUNT,)),
    ]
    return pl.pallas_call(
        kernel,
        out_shape=(wide32, wide32, wide16, wide16, wide16, wide16),
        in_specs=[pl.BlockSpec(memory_space=pltpu.VMEM)] * 2 + [any_spec] * 8,
        out_specs=(any_spec,) * 6,
        scratch_shapes=scratch,
        compiler_params=pltpu.CompilerParams(
            collective_id=0, has_side_effects=True, vmem_limit_bytes=60 * 1024 * 1024
        ),
        cost_estimate=pl.CostEstimate(
            flops=4_000_000_000, bytes_accessed=11_000_000, transcendentals=131072
        ),
    )(*arrays)


def solution(mesh):
    rows = P(("dp", "tensor"), None)
    return jax.shard_map(
        per_device, mesh=mesh, in_specs=(rows,) * 10, out_specs=(rows,) * 6, check_vma=False
    )
```

```python
import math

import jax
import jax.numpy as jnp
from jax import lax
from jax.experimental import pallas as pl
from jax.experimental.pallas import tpu as pltpu
from jax.sharding import PartitionSpec as P

TOKENS = 512
D = 3072
HID = 96
PAD = 128
PARTS = 3
SIZE = {"y": 4, "x": 4, "z": 8}
AXES = ("y", "x", "z")
GROUP = 8
WIDE = D // GROUP
NEAR = (2, 1, 3)
PARTS = (("y", "x"), ("x", "y"))
OFFSETS = (0, 1, 7, 6, 2, 3, 5, 4)
PAIRS = ((0, 0, 2), (1, 2, 2), (0, 4, 2), (1, 6, 2))
SETS = ((0, 0, 1), (0, 1, 1), (1, 2, 1), (1, 3, 1), (0, 4, 2), (1, 6, 2))
GATHER_COUNT = 7 + 6 * 15 + 4
SCATTER_COUNT = 4 * 15 + 7

beta_first = 0.965
beta_second = 0.99
gamma_scale = 0.01
ratio_floor = 0.01
root_half = 0.7071067811865476
inv_root_tau = 0.3989422804014327

F32 = jnp.float32
BF16 = jnp.bfloat16
MESH = pl.DeviceIdType.MESH


def gelu_parts(pre_act):
    normal_cdf = 0.5 * (1.0 + lax.erf(pre_act * root_half))
    density = jnp.exp(-0.5 * pre_act * pre_act) * inv_root_tau
    return (
        pre_act * normal_cdf,
        normal_cdf + pre_act * density,
        density * (2.0 - pre_act * pre_act),
    )


def refresh(moment, curve, grad, hvp, tangent):
    moment_f = beta_first * moment.astype(F32) + (1.0 - beta_first) * grad
    curve_f = beta_second * curve.astype(F32) + (1.0 - beta_second) * tangent.astype(F32) * hvp
    step = jnp.clip(moment_f / jnp.maximum(gamma_scale * curve_f, ratio_floor), -1.0, 1.0)
    return step, moment_f.astype(BF16), curve_f.astype(BF16)


def wrap(value, size):
    return lax.rem(value + size, size)


class Here:
    def __init__(self):
        dp = lax.axis_index("dp")
        tensor = lax.axis_index("tensor")
        self.core = lax.rem(tensor, 2)
        self.pos = {
            "x": lax.rem(lax.div(dp, 8), 4),
            "z": lax.rem(dp, 8),
            "y": lax.div(tensor, 2) * 2 + lax.div(dp, 32),
        }
        self.me = self.core * 4 + self.pos["y"]
        self.steps = {
            (axis, by): wrap(self.pos[axis] + by, SIZE[axis])
            for axis in AXES
            for by in range(SIZE[axis])
        }
        self.devices = {
            key: self.device({**self.pos, key[0]: spot}, self.core)
            for key, spot in self.steps.items()
            if key[1]
        }
        self.sibling = self.device(self.pos, 1 - self.core)

    def device(self, pos, core):
        y = pos["y"]
        return (
            lax.rem(y, 2) * 32 + pos["x"] * 8 + pos["z"],
            lax.div(y, 2) * 2 + core,
        )

    def member(self, by):
        spot = lax.rem(self.me + by, GROUP)
        return self.device({**self.pos, "y": lax.rem(spot, 4)}, lax.div(spot, 4))

    def step(self, axis, by):
        return self.steps[(axis, by % SIZE[axis])]

    def beside(self, axis, by):
        return self.devices[(axis, by)]


def place(where):
    return tuple(where[axis] for axis in AXES)


def gather(buffer, here, sets, send_sems, recv_sems, sent, keep=None):
    mine = buffer.at[here.core]
    other = buffer.at[1 - here.core]

    def copy(index, source, into, target):
        return pltpu.make_async_remote_copy(
            src_ref=source,
            dst_ref=into,
            send_sem=send_sems.at[index],
            recv_sem=recv_sems.at[index],
            device_id=target,
            device_id_type=MESH,
        )

    def start(index, source, into, target):
        made = copy(index, source, into, target)
        made.start()
        sent.append(made)

    def set_block(q, m, f):
        part, row, rows = sets[q]
        middle, final = PARTS[part]
        where = {
            middle: here.step(middle, -m),
            final: here.step(final, -f),
            "z": pl.ds(row, rows),
        }
        return mine.at[place(where)]

    def launch(q):
        middle, final = PARTS[sets[q][0]]
        own = set_block(q, 0, 0)
        for m in NEAR:
            start(7 + q * 15 + m - 1, own, own, here.beside(middle, m))
        for f in NEAR:
            start(10 + q * 15 + f - 1, own, own, here.beside(final, f))

    def arrive(*offsets):
        for offset in offsets:
            came = mine.at[place({**here.pos, "z": OFFSETS.index(offset)})]
            copy(7 - offset, came, came, here.sibling).wait_recv()

    def forward(q):
        final = PARTS[sets[q][0]][1]
        for m in (1, 3, 2):
            came = set_block(q, m, 0)
            copy(7 + q * 15 + m - 1, came, came, here.sibling).wait_recv()
            for f in NEAR:
                start(13 + q * 15 + (m - 1) * 3 + f - 1, came, came, here.beside(final, f))

    def finish(q):
        for m in (0, 1, 3, 2):
            for f in (1, 3, 2):
                index = (10 if m == 0 else 13 + (m - 1) * 3) + q * 15 + f - 1
                came = set_block(q, m, f)
                copy(index, came, came, here.sibling).wait_recv()

    def hand_on(number):
        row = PAIRS[number][1]
        ref = mine.at[:, :, row : row + 2]
        start(97 + number, ref, ref, here.sibling)

    own = mine.at[place({**here.pos, "z": 0})]
    for by in (1, 7, 2, 6, 3, 5, 4):
        into = mine.at[place({**here.pos, "z": OFFSETS.index(8 - by)})]
        start(by - 1, own, into, here.beside("z", by))
    if len(sets) == 6:
        launch(0)
        yield
        arrive(1)
        launch(1)
        arrive(7)
        launch(2)
        arrive(6)
        launch(3)
        forward(0)
        arrive(2, 3)
        launch(4)
        arrive(5, 4)
        launch(5)
        for q in (1, 2, 3, 4, 5):
            forward(q)
        completing = (1, 3, 4, 5)
    else:
        yield
        arrive(1)
        launch(0)
        arrive(7, 6)
        launch(1)
        arrive(2, 3)
        launch(2)
        arrive(5, 4)
        launch(3)
        for q in range(4):
            forward(q)
        completing = (0, 1, 2, 3)
    for q in range(len(sets)):
        finish(q)
        if q in completing:
            hand_on(completing.index(q))
            if keep is not None:
                keep(completing.index(q), here.core)
    for number, (_, row, rows) in enumerate(PAIRS):
        came = other.at[:, :, row : row + rows]
        copy(97 + number, came, came, here.sibling).wait_recv()
        if keep is not None:
            keep(number, 1 - here.core)


class Scatter:
    def __init__(self, sums, boxes, here, send_sems, recv_sems, sent):
        self.sums, self.boxes, self.here = sums, boxes, here
        self.send_sems, self.recv_sems, self.sent = send_sems, recv_sems, sent

    def copy(self, index, source, into, target):
        return pltpu.make_async_remote_copy(
            src_ref=source,
            dst_ref=into,
            send_sem=self.send_sems.at[index],
            recv_sem=self.recv_sems.at[index],
            device_id=target,
            device_id_type=MESH,
        )

    def start(self, *what):
        made = self.copy(*what)
        made.start()
        self.sent.append(made)

    def rows(self, q):
        return pl.ds(PAIRS[q][1], PAIRS[q][2])

    def piece(self, q, by_first, by_second):
        second, first = PARTS[PAIRS[q][0]]
        where = {
            first: self.here.step(first, by_first),
            second: self.here.step(second, by_second),
            "z": self.rows(q),
        }
        return place(where)

    def first_x(self, q, by, by_second):
        self.start(
            q * 15 + (by - 1) * 4 + by_second,
            self.sums.at[self.piece(q, by, by_second)],
            self.boxes[0].at[by - 1, by_second, self.rows(q)],
            self.here.beside("x", by),
        )

    def first_y(self, q, by):
        self.start(
            q * 15 + by - 1,
            self.sums.at[self.here.step("y", by), :, self.rows(q)],
            self.boxes[0].at[by - 1, :, self.rows(q)],
            self.here.beside("y", by),
        )

    def came(self, index, into):
        self.copy(index, into, into, self.here.sibling).wait_recv()

    def second(self, q, by_second, fresh):
        where = self.piece(q, 0, by_second)
        total = self.sums[where].astype(F32)
        rows = self.rows(q)
        for by in (1, 3, 2):
            if PAIRS[q][0] == 0:
                into = (by - 1, by_second, rows)
                self.came(q * 15 + (by - 1) * 4 + by_second, self.boxes[0].at[into])
            else:
                into = (by - 1, self.here.step("x", by_second), rows)
                if fresh:
                    self.came(q * 15 + by - 1, self.boxes[0].at[by - 1, :, rows])
            total = total + self.boxes[0][into].astype(F32)
        if by_second:
            self.sums[where] = total.astype(BF16)
            self.start(
                q * 15 + 12 + by_second - 1,
                self.sums.at[where],
                self.boxes[1].at[by_second - 1, rows],
                self.here.beside(PARTS[PAIRS[q][0]][0], by_second),
            )
            return
        for by in (1, 3, 2):
            into = (by - 1, rows)
            self.came(q * 15 + 12 + by - 1, self.boxes[1].at[into])
            total = total + self.boxes[1][into].astype(F32)
        self.sums[where] = total.astype(BF16)

    def third(self, *offsets):
        for by in offsets:
            self.start(
                60 + by - 1,
                self.sums.at[place({**self.here.pos, "z": OFFSETS.index(by)})],
                self.boxes[2].at[by - 1],
                self.here.beside("z", by),
            )

    def total(self):
        total = self.sums[place({**self.here.pos, "z": 0})].astype(F32)
        for by in (4, 3, 5, 2, 6, 1, 7):
            self.came(60 + by - 1, self.boxes[2].at[by - 1])
            total = total + self.boxes[2][by - 1].astype(F32)
        return total


def kernel(
    tokens,
    target,
    master_up,
    master_down,
    tangent_up,
    tangent_down,
    tokens_out,
    residuals_out,
    both_t,
    grads_t,
    v_master_up,
    v_master_down,
    v_tangent_up,
    v_tangent_down,
    group,
    folded,
    all_tokens,
    weights_up,
    weights_down,
    acc,
    both,
    slopes_ref,
    bend_ref,
    outgoing,
    incoming,
    sums,
    residuals,
    *rest,
):
    boxes = rest[:3]
    in_sems, out_sems, pair_send, pair_recv, group_send, group_recv = rest[3:9]
    first_send, first_recv, scatter_send, scatter_recv, second_send, second_recv = rest[9:]

    here = Here()
    core, pos, me = here.core, here.pos, here.me
    sent = []

    loads = []
    pairs = (
        (master_up, v_master_up),
        (tangent_up, v_tangent_up),
        (master_down, v_master_down),
        (tangent_down, v_tangent_down),
    )
    for number, (source, into) in enumerate(pairs):
        made = pltpu.make_async_copy(source, into, in_sems.at[number])
        made.start()
        loads.append(made)

    barrier = pltpu.get_barrier_semaphore()
    peers = [here.member(by) for by in range(1, GROUP)]
    peers += [here.beside("x", by) for by in range(1, 4)]
    peers += [here.beside("z", by) for by in range(1, 8)]
    for peer in peers:
        pl.semaphore_signal(barrier, inc=1, device_id=peer, device_id_type=MESH)

    def fold(rows):
        rows = rows.astype(F32)
        pieces = [rows[:, k * WIDE : (k + 1) * WIDE] for k in range(GROUP)]
        return jnp.concatenate(pieces, axis=0).astype(BF16)

    folded[core, pos["y"], pos["x"], 0] = fold(tokens[...])
    group[me] = fold(target[...])

    loads[0].wait()
    loads[1].wait()
    zeros_up = jnp.zeros((PAD - HID, 768), BF16)
    for k in range(4):
        columns = slice(k * 768, (k + 1) * 768)
        weights_up[k, 0:HID] = v_master_up[:, columns].astype(BF16)
        weights_up[k, HID:PAD] = zeros_up
        weights_up[k, PAD : PAD + HID] = v_tangent_up[:, columns]
        weights_up[k, PAD + HID :] = zeros_up
    pl.semaphore_wait(barrier, len(peers))

    first = gather(folded, here, PAIRS, first_send, first_recv, sent)
    next(first)

    def group_copy(by, spot):
        return pltpu.make_async_remote_copy(
            src_ref=group.at[spot],
            dst_ref=group.at[spot],
            send_sem=group_send.at[by],
            recv_sem=group_recv.at[by],
            device_id=here.member(by),
            device_id_type=MESH,
        )

    for by in range(1, GROUP):
        made = group_copy(by, me)
        made.start()
        sent.append(made)

    loads[2].wait()
    loads[3].wait()
    zeros_low = jnp.zeros((PAD - HID, 2 * WIDE), BF16)
    zeros_half = jnp.zeros((HID, WIDE), BF16)
    for spot in range(GROUP):
        columns = slice(spot * WIDE, (spot + 1) * WIDE)
        weight = v_master_down[:, columns].astype(BF16)
        weights_down[spot, 0:HID, 0:WIDE] = weight
        weights_down[spot, 0:HID, WIDE:] = v_tangent_down[:, columns]
        weights_down[spot, HID:PAD] = zeros_low
        weights_down[spot, PAD : PAD + HID, 0:WIDE] = zeros_half
        weights_down[spot, PAD : PAD + HID, WIDE:] = weight
        weights_down[spot, PAD + HID :] = zeros_low

    for _ in first:
        pass

    row = lax.broadcasted_iota(jnp.int32, (128, 128), 0)
    column = lax.broadcasted_iota(jnp.int32, (128, 128), 1)
    token = lax.rem(row, 16)
    pick = column == lax.div(token, 2) * 16 + lax.div(row, 16) * 2 + lax.rem(token, 2)
    pick = pick.astype(F32).astype(BF16)

    @pl.loop(0, 4)
    def _(x):
        for z in range(8):
            blocks = folded[:, :, x, z].reshape(128, WIDE)
            rows = jnp.dot(pick, blocks, preferred_element_type=F32).astype(BF16)
            all_tokens[:, x, z] = rows.reshape(GROUP, 16, WIDE)

    stores = [pltpu.make_async_copy(all_tokens, tokens_out, out_sems.at[0])]
    stores[0].start()

    acc[...] = jnp.zeros_like(acc)

    @pl.loop(0, 4)
    def _(k):
        blocks = [all_tokens[2 * k + lower].reshape(TOKENS, WIDE) for lower in range(2)]
        acc[...] += lax.dot_general(
            jnp.concatenate(blocks, axis=1),
            weights_up[k],
            (((1,), (1,)), ((), ())),
            preferred_element_type=F32,
        )

    @pl.loop(0, 4)
    def _(x):
        span = pl.ds(pl.multiple_of(x * 128, 128), 128)
        pre_tangent = acc[span, PAD:]
        activated, slopes, bending = gelu_parts(acc[span, :PAD])
        slopes_ref[span] = slopes
        bend_ref[span] = bending * pre_tangent
        pair = jnp.concatenate([activated, slopes * pre_tangent], axis=1)
        both[x] = pair.astype(BF16).reshape(8, 16, 2 * PAD)

    def pair_copy(far, by):
        return pltpu.make_async_remote_copy(
            src_ref=outgoing.at[far, by],
            dst_ref=incoming.at[far, by],
            send_sem=pair_send.at[far, by],
            recv_sem=pair_recv.at[far, by],
            device_id=here.sibling,
            device_id_type=MESH,
        )

    turns = (1, 3, 2, 0)
    shape = (4, 4, 16, 2 * WIDE)

    def product(far, spot):
        left = both[:, 4 * far : 4 * far + 4].reshape(TOKENS // 2, 2 * PAD)
        return jnp.dot(left, weights_down[spot], preferred_element_type=F32)

    for far in (1, 0):
        for by in turns:
            spot = (1 - core) * 4 + here.step("y", by)
            outgoing[far, by] = product(far, spot).astype(BF16).reshape(shape)
            made = pair_copy(far, by)
            made.start()
            sent.append(made)

    scatter = Scatter(sums, boxes, here, scatter_send, scatter_recv, sent)
    for far in (1, 0):
        for by in turns:
            pair_copy(far, by).wait_recv()
            y = here.step("y", by)
            block = product(far, core * 4 + y)
            block = block + incoming[far, by].astype(F32).reshape(TOKENS // 2, 2 * WIDE)
            sums[y, :, 4 * far : 4 * far + 4] = block.astype(BF16).reshape(shape)
            for to in NEAR:
                scatter.first_x(2 * far, to, by)
            if by:
                scatter.first_y(2 * far + 1, by)

    both_t[...] = both[...].reshape(TOKENS, 2 * PAD).astype(F32).T.astype(BF16)
    for by in turns:
        for q in (2, 3):
            scatter.second(q, by, by == turns[0])
    scatter.third(4, 3, 5, 2)
    for by in turns:
        for q in (1, 0):
            scatter.second(q, by, by == turns[0])
            if by == 0:
                scatter.third(*((6, 7) if q else (1,)))
    total = scatter.total()

    for by in range(1, GROUP):
        group_copy(by, lax.rem(me + GROUP - by, GROUP)).wait_recv()
    row = lax.broadcasted_iota(jnp.int32, (16, 128), 0)
    column = lax.broadcasted_iota(jnp.int32, (16, 128), 1)
    pick = (column == lax.div(row, 2) * 16 + me * 2 + lax.rem(row, 2)).astype(F32).astype(BF16)
    goal = jnp.dot(pick, group[...].reshape(128, WIDE), preferred_element_type=F32)
    pair = jnp.concatenate([total[:, WIDE:], total[:, :WIDE] - goal], axis=1)
    residuals[core, pos["y"], pos["x"], 0] = pair.astype(BF16)

    def keep(number, core):
        row = PAIRS[number][1]
        made = pltpu.make_async_copy(
            residuals.at[core, :, :, row : row + 2],
            residuals_out.at[core, :, :, row : row + 2],
            out_sems.at[len(stores)],
        )
        made.start()
        stores.append(made)

    earlier = list(sent)
    sent.clear()
    last = gather(residuals, here, SETS, second_send, second_recv, sent, keep)
    next(last)
    for made in earlier:
        made.wait_send()
    for _ in last:
        pass

    acc[...] = jnp.zeros_like(acc)

    @pl.loop(0, GROUP)
    def _(spot):
        acc[...] += lax.dot_general(
            residuals[lax.div(spot, 4), lax.rem(spot, 4)].reshape(TOKENS, 2 * WIDE),
            weights_down[spot],
            (((1,), (1,)), ((), ())),
            preferred_element_type=F32,
        )

    for k in range(4):
        span = slice(k * 128, (k + 1) * 128)
        back_dot, back_grad = acc[span, :PAD], acc[span, PAD:]
        slopes = slopes_ref[span]
        grad_pre = (back_grad * slopes).T.astype(BF16)
        grad_pre_dot = (back_dot * slopes + back_grad * bend_ref[span]).T.astype(BF16)
        grads_t[0:PAD, span] = grad_pre
        grads_t[PAD:, span] = grad_pre_dot

    for made in stores:
        made.wait()
    for made in sent:
        made.wait_send()


def update(
    grads_t,
    both_t,
    tokens,
    residuals,
    tangent_up,
    tangent_down,
    moment_up,
    moment_down,
    curve_up,
    curve_down,
    step_up,
    step_down,
    moment_up_next,
    moment_down_next,
    curve_up_next,
    curve_down_next,
):
    loss_scale = 1.0 / math.sqrt(TOKENS)
    wide = [tokens[k].reshape(TOKENS, WIDE) for k in range(2)]
    up = jnp.dot(grads_t[...], jnp.concatenate(wide, axis=1), preferred_element_type=F32)
    step_up[...], moment_up_next[...], curve_up_next[...] = refresh(
        moment_up[...],
        curve_up[...],
        loss_scale * up[:HID],
        loss_scale * up[PAD : PAD + HID],
        tangent_up[...],
    )
    grad, hvp = [], []
    for k in range(2):
        down = jnp.dot(
            both_t[...],
            residuals[k].reshape(TOKENS, 2 * WIDE),
            preferred_element_type=F32,
        )
        grad.append(down[:HID, WIDE:])
        hvp.append(down[:HID, :WIDE] + down[PAD : PAD + HID, WIDE:])
    step_down[...], moment_down_next[...], curve_down_next[...] = refresh(
        moment_down[...],
        curve_down[...],
        loss_scale * jnp.concatenate(grad, axis=1),
        loss_scale * jnp.concatenate(hvp, axis=1),
        tangent_down[...],
    )


def per_device(
    tokens,
    target,
    master_up,
    master_down,
    tangent_up,
    tangent_down,
    moment_up,
    moment_down,
    curve_up,
    curve_down,
):
    wide32 = jax.ShapeDtypeStruct((HID, D), F32)
    wide16 = jax.ShapeDtypeStruct((HID, D), BF16)
    blocks = (4, 4, 8, 16)
    any_spec = pl.BlockSpec(memory_space=pl.ANY)
    vmem_spec = pl.BlockSpec(memory_space=pltpu.VMEM)
    scratch = [pltpu.VMEM((HID, D), F32)] * 2 + [pltpu.VMEM((HID, D), BF16)] * 2
    scratch += [
        pltpu.VMEM((GROUP, 16, WIDE), BF16),
        pltpu.VMEM((2,) + blocks + (WIDE,), BF16),
        pltpu.VMEM((GROUP, 4, 8, 16, WIDE), BF16),
        pltpu.VMEM((4, 2 * PAD, 768), BF16),
        pltpu.VMEM((GROUP, 2 * PAD, 2 * WIDE), BF16),
        pltpu.VMEM((TOKENS, 2 * PAD), F32),
        pltpu.VMEM((4, 8, 16, 2 * PAD), BF16),
        pltpu.VMEM((TOKENS, PAD), F32),
        pltpu.VMEM((TOKENS, PAD), F32),
        pltpu.VMEM((2, 4, 4, 4, 16, 2 * WIDE), BF16),
        pltpu.VMEM((2, 4, 4, 4, 16, 2 * WIDE), BF16),
        pltpu.VMEM(blocks + (2 * WIDE,), BF16),
        pltpu.VMEM((2,) + blocks + (2 * WIDE,), BF16),
        pltpu.VMEM((3, 4, 8, 16, 2 * WIDE), BF16),
        pltpu.VMEM((3, 8, 16, 2 * WIDE), BF16),
        pltpu.VMEM((7, 16, 2 * WIDE), BF16),
    ]
    dma = pltpu.SemaphoreType.DMA
    scratch += [
        dma((4,)),
        dma((9,)),
        dma((2, 4)),
        dma((2, 4)),
        dma((GROUP,)),
        dma((GROUP,)),
        dma((GATHER_COUNT,)),
        dma((GATHER_COUNT,)),
        dma((SCATTER_COUNT,)),
        dma((SCATTER_COUNT,)),
        dma((GATHER_COUNT,)),
        dma((GATHER_COUNT,)),
    ]
    all_tokens, residuals, both_t, grads_t = pl.pallas_call(
        kernel,
        out_shape=(
            jax.ShapeDtypeStruct((GROUP, 4, 8, 16, WIDE), BF16),
            jax.ShapeDtypeStruct((2,) + blocks + (2 * WIDE,), BF16),
            jax.ShapeDtypeStruct((2 * PAD, TOKENS), BF16),
            jax.ShapeDtypeStruct((2 * PAD, TOKENS), BF16),
        ),
        in_specs=[vmem_spec] * 2 + [any_spec] * 4,
        out_specs=(any_spec, any_spec, vmem_spec, vmem_spec),
        scratch_shapes=scratch,
        compiler_params=pltpu.CompilerParams(
            collective_id=0, has_side_effects=True, vmem_limit_bytes=62 * 1024 * 1024
        ),
        cost_estimate=pl.CostEstimate(
            flops=3_000_000_000, bytes_accessed=16_000_000, transcendentals=131072
        ),
    )(tokens, target, master_up, master_down, tangent_up, tangent_down)
    residuals = residuals.reshape((GROUP, 4, 8, 16, 2 * WIDE))
    whole = pl.BlockSpec((2 * PAD, TOKENS), lambda spot: (0, 0))
    part = pl.BlockSpec((HID, 2 * WIDE), lambda spot: (0, spot))
    return pl.pallas_call(
        update,
        grid=(GROUP // 2,),
        out_shape=(wide32, wide32, wide16, wide16, wide16, wide16),
        in_specs=[
            whole,
            whole,
            pl.BlockSpec((2, 4, 8, 16, WIDE), lambda spot: (spot, 0, 0, 0, 0)),
            pl.BlockSpec((2, 4, 8, 16, 2 * WIDE), lambda spot: (spot, 0, 0, 0, 0)),
        ]
        + [part] * 6,
        out_specs=(part,) * 6,
        compiler_params=pltpu.CompilerParams(vmem_limit_bytes=62 * 1024 * 1024),
        cost_estimate=pl.CostEstimate(
            flops=1_500_000_000, bytes_accessed=18_000_000, transcendentals=0
        ),
    )(
        grads_t,
        both_t,
        all_tokens,
        residuals,
        tangent_up,
        tangent_down,
        moment_up,
        moment_down,
        curve_up,
        curve_down,
    )


def solution(mesh):
    rows = P(("dp", "tensor"), None)
    return jax.shard_map(
        per_device, mesh=mesh, in_specs=(rows,) * 10, out_specs=(rows,) * 6, check_vma=False
    )
```

```python
import math

import jax
import jax.numpy as jnp
from jax import lax
from jax.experimental import pallas as pl
from jax.experimental.pallas import tpu as pltpu
from jax.sharding import PartitionSpec as P

TOKENS = 512
D = 3072
HID = 96
PAD = 128
PARTS = 3
SIZE = {"y": 4, "x": 4, "z": 8}
AXES = ("y", "x", "z")
GROUP = 8
WIDE = D // GROUP
NEAR = (2, 1, 3)
PARTS = (("y", "x"), ("x", "y"))
OFFSETS = (0, 1, 7, 6, 2, 3, 5, 4)
PAIRS = ((0, 0, 2), (1, 2, 2), (0, 4, 2), (1, 6, 2))
SETS = ((0, 0, 1), (0, 1, 1), (1, 2, 1), (1, 3, 1), (0, 4, 2), (1, 6, 2))
MAIN = 640
SIDE = pl.ds(MAIN, 2 * WIDE - MAIN)
GATHER_COUNT = 7 + 6 * 15 + 4 + 1 + 3 + 3 + 7
SCATTER_COUNT = 4 * 15 + 7 + 7 + 3 + 3

beta_first = 0.965
beta_second = 0.99
gamma_scale = 0.01
ratio_floor = 0.01
root_half = 0.7071067811865476
inv_root_tau = 0.3989422804014327

F32 = jnp.float32
BF16 = jnp.bfloat16
MESH = pl.DeviceIdType.MESH


def gelu_parts(pre_act):
    normal_cdf = 0.5 * (1.0 + lax.erf(pre_act * root_half))
    density = jnp.exp(-0.5 * pre_act * pre_act) * inv_root_tau
    return (
        pre_act * normal_cdf,
        normal_cdf + pre_act * density,
        density * (2.0 - pre_act * pre_act),
    )


def refresh(moment, curve, grad, hvp, tangent):
    moment_f = beta_first * moment.astype(F32) + (1.0 - beta_first) * grad
    curve_f = beta_second * curve.astype(F32) + (1.0 - beta_second) * tangent.astype(F32) * hvp
    step = jnp.clip(moment_f / jnp.maximum(gamma_scale * curve_f, ratio_floor), -1.0, 1.0)
    return step, moment_f.astype(BF16), curve_f.astype(BF16)


def wrap(value, size):
    return lax.rem(value + size, size)


class Here:
    def __init__(self):
        dp = lax.axis_index("dp")
        tensor = lax.axis_index("tensor")
        self.core = lax.rem(tensor, 2)
        self.pos = {
            "x": lax.rem(lax.div(dp, 8), 4),
            "z": lax.rem(dp, 8),
            "y": lax.div(tensor, 2) * 2 + lax.div(dp, 32),
        }
        self.me = self.core * 4 + self.pos["y"]
        self.steps = {
            (axis, by): wrap(self.pos[axis] + by, SIZE[axis])
            for axis in AXES
            for by in range(SIZE[axis])
        }
        self.devices = {
            key: self.device({**self.pos, key[0]: spot}, self.core)
            for key, spot in self.steps.items()
            if key[1]
        }
        self.sibling = self.device(self.pos, 1 - self.core)

    def device(self, pos, core):
        y = pos["y"]
        return (
            lax.rem(y, 2) * 32 + pos["x"] * 8 + pos["z"],
            lax.div(y, 2) * 2 + core,
        )

    def member(self, by):
        spot = lax.rem(self.me + by, GROUP)
        return self.device({**self.pos, "y": lax.rem(spot, 4)}, lax.div(spot, 4))

    def step(self, axis, by):
        return self.steps[(axis, by % SIZE[axis])]

    def beside(self, axis, by):
        return self.devices[(axis, by)]


def place(where):
    return tuple(where[axis] for axis in AXES)


def gather(buffer, here, sets, send_sems, recv_sems, sent, keep=None):
    side = keep is not None
    columns = pl.ds(0, MAIN if side else WIDE)
    mine = buffer.at[here.core]
    other = buffer.at[1 - here.core]

    def copy(index, source, into, target):
        return pltpu.make_async_remote_copy(
            src_ref=source,
            dst_ref=into,
            send_sem=send_sems.at[index],
            recv_sem=recv_sems.at[index],
            device_id=target,
            device_id_type=MESH,
        )

    def start(index, source, into, target):
        made = copy(index, source, into, target)
        made.start()
        sent.append(made)

    def set_block(q, m, f):
        part, row, rows = sets[q]
        middle, final = PARTS[part]
        where = {
            middle: here.step(middle, -m),
            final: here.step(final, -f),
            "z": pl.ds(row, rows),
        }
        return mine.at[place(where) + (slice(None), columns)]

    def launch(q):
        middle, final = PARTS[sets[q][0]]
        own = set_block(q, 0, 0)
        for m in NEAR:
            start(7 + q * 15 + m - 1, own, own, here.beside(middle, m))
        for f in NEAR:
            start(10 + q * 15 + f - 1, own, own, here.beside(final, f))

    def arrive(*offsets):
        for offset in offsets:
            where = place({**here.pos, "z": OFFSETS.index(offset)})
            came = mine.at[where + (slice(None), columns)]
            copy(7 - offset, came, came, here.sibling).wait_recv()

    def forward(q):
        final = PARTS[sets[q][0]][1]
        for m in (1, 3, 2):
            came = set_block(q, m, 0)
            copy(7 + q * 15 + m - 1, came, came, here.sibling).wait_recv()
            for f in NEAR:
                start(13 + q * 15 + (m - 1) * 3 + f - 1, came, came, here.beside(final, f))

    def finish(q):
        for m in (0, 1, 3, 2):
            for f in (1, 3, 2):
                index = (10 if m == 0 else 13 + (m - 1) * 3) + q * 15 + f - 1
                came = set_block(q, m, f)
                copy(index, came, came, here.sibling).wait_recv()

    def hand_on(number):
        row = PAIRS[number][1]
        ref = mine.at[:, :, row : row + 2, :, columns]
        start(97 + number, ref, ref, here.sibling)

    here_y, here_x = here.pos["y"], here.pos["x"]

    def side_x():
        ref = mine.at[here_y, here_x, 0, :, SIDE]
        for by in NEAR:
            start(102 + by - 1, ref, ref, here.beside("x", by))

    def side_y():
        for by in NEAR:
            ref = mine.at[here_y, here.step("x", -by), 0, :, SIDE]
            copy(102 + by - 1, ref, ref, here.sibling).wait_recv()
        ref = mine.at[here_y, :, 0, :, SIDE]
        for by in NEAR:
            start(105 + by - 1, ref, ref, here.beside("y", by))

    def side_z():
        for by in NEAR:
            ref = mine.at[here.step("y", -by), :, 0, :, SIDE]
            copy(105 + by - 1, ref, ref, here.sibling).wait_recv()
        for by in (4, 3, 5, 2, 6, 1, 7):
            into = mine.at[:, :, OFFSETS.index(8 - by), :, SIDE]
            start(108 + by - 1, mine.at[:, :, 0, :, SIDE], into, here.beside("z", by))

    def side_end():
        for by in (1, 7, 2, 6, 3, 5, 4):
            ref = mine.at[:, :, OFFSETS.index(8 - by), :, SIDE]
            copy(108 + by - 1, ref, ref, here.sibling).wait_recv()
        ref = mine.at[:, :, :, :, SIDE]
        start(101, ref, ref, here.sibling)
        keep(None, here.core)

    if side:
        side_x()
    own = mine.at[place({**here.pos, "z": 0}) + (slice(None), columns)]
    for by in (1, 7, 2, 6, 3, 5, 4):
        into = mine.at[place({**here.pos, "z": OFFSETS.index(8 - by)}) + (slice(None), columns)]
        start(by - 1, own, into, here.beside("z", by))
    if len(sets) == 6:
        launch(0)
        yield
        arrive(1)
        launch(1)
        side_y()
        arrive(7)
        launch(2)
        arrive(6)
        launch(3)
        forward(0)
        side_z()
        arrive(2, 3)
        launch(4)
        arrive(5, 4)
        launch(5)
        for q in (1, 2, 3, 4, 5):
            forward(q)
        completing = (1, 3, 4, 5)
    else:
        yield
        arrive(1)
        launch(0)
        arrive(7, 6)
        launch(1)
        arrive(2, 3)
        launch(2)
        arrive(5, 4)
        launch(3)
        for q in range(4):
            forward(q)
        completing = (0, 1, 2, 3)
    for q in range(len(sets)):
        finish(q)
        if side and q == 3:
            side_end()
        if q in completing:
            hand_on(completing.index(q))
            if keep is not None:
                keep(completing.index(q), here.core)
    for number, (_, row, rows) in enumerate(PAIRS):
        came = other.at[:, :, row : row + rows, :, columns]
        copy(97 + number, came, came, here.sibling).wait_recv()
        if keep is not None:
            keep(number, 1 - here.core)
    if side:
        came = other.at[:, :, :, :, SIDE]
        copy(101, came, came, here.sibling).wait_recv()
        keep(None, 1 - here.core)


class Scatter:
    def __init__(self, sums, boxes, here, send_sems, recv_sems, sent):
        self.sums, self.boxes, self.here = sums, boxes, here
        self.send_sems, self.recv_sems, self.sent = send_sems, recv_sems, sent

    def copy(self, index, source, into, target):
        return pltpu.make_async_remote_copy(
            src_ref=source,
            dst_ref=into,
            send_sem=self.send_sems.at[index],
            recv_sem=self.recv_sems.at[index],
            device_id=target,
            device_id_type=MESH,
        )

    def start(self, *what):
        made = self.copy(*what)
        made.start()
        self.sent.append(made)

    def rows(self, q):
        return pl.ds(PAIRS[q][1], PAIRS[q][2])

    def piece(self, q, by_first, by_second):
        second, first = PARTS[PAIRS[q][0]]
        where = {
            first: self.here.step(first, by_first),
            second: self.here.step(second, by_second),
            "z": self.rows(q),
        }
        return place(where) + (slice(None), pl.ds(0, MAIN))

    def first_x(self, q, by, by_second):
        self.start(
            q * 15 + (by - 1) * 4 + by_second,
            self.sums.at[self.piece(q, by, by_second)],
            self.boxes[0].at[by - 1, by_second, self.rows(q)],
            self.here.beside("x", by),
        )

    def first_y(self, q, by):
        self.start(
            q * 15 + by - 1,
            self.sums.at[self.here.step("y", by), :, self.rows(q), :, pl.ds(0, MAIN)],
            self.boxes[0].at[by - 1, :, self.rows(q)],
            self.here.beside("y", by),
        )

    def came(self, index, into):
        self.copy(index, into, into, self.here.sibling).wait_recv()

    def second(self, q, by_second, fresh):
        where = self.piece(q, 0, by_second)
        total = self.sums[where].astype(F32)
        rows = self.rows(q)
        for by in (1, 3, 2):
            if PAIRS[q][0] == 0:
                into = (by - 1, by_second, rows)
                self.came(q * 15 + (by - 1) * 4 + by_second, self.boxes[0].at[into])
            else:
                into = (by - 1, self.here.step("x", by_second), rows)
                if fresh:
                    self.came(q * 15 + by - 1, self.boxes[0].at[by - 1, :, rows])
            total = total + self.boxes[0][into].astype(F32)
        if by_second:
            self.sums[where] = total.astype(BF16)
            self.start(
                q * 15 + 12 + by_second - 1,
                self.sums.at[where],
                self.boxes[1].at[by_second - 1, rows],
                self.here.beside(PARTS[PAIRS[q][0]][0], by_second),
            )
            return
        for by in (1, 3, 2):
            into = (by - 1, rows)
            self.came(q * 15 + 12 + by - 1, self.boxes[1].at[into])
            total = total + self.boxes[1][into].astype(F32)
        self.sums[where] = total.astype(BF16)

    def third(self, *offsets):
        for by in offsets:
            self.start(
                60 + by - 1,
                self.sums.at[self.own(OFFSETS.index(by))],
                self.boxes[2].at[by - 1],
                self.here.beside("z", by),
            )

    def own(self, row):
        return place({**self.here.pos, "z": row}) + (slice(None), pl.ds(0, MAIN))

    def side_z(self, *offsets):
        for by in offsets:
            self.start(
                67 + by - 1,
                self.sums.at[:, :, OFFSETS.index(by), :, SIDE],
                self.boxes[3].at[by - 1],
                self.here.beside("z", by),
            )

    def side_y(self):
        total = self.sums[:, :, 0, :, SIDE].astype(F32)
        for by in (1, 7, 2, 6, 3, 5, 4):
            self.came(67 + by - 1, self.boxes[3].at[by - 1])
            total = total + self.boxes[3][by - 1].astype(F32)
        self.sums[:, :, 0, :, SIDE] = total.astype(BF16)
        for by in NEAR:
            self.start(
                74 + by - 1,
                self.sums.at[self.here.step("y", by), :, 0, :, SIDE],
                self.boxes[4].at[by - 1],
                self.here.beside("y", by),
            )

    def side_x(self):
        y = self.here.pos["y"]
        total = self.sums[y, :, 0, :, SIDE].astype(F32)
        for by in (1, 3, 2):
            self.came(74 + by - 1, self.boxes[4].at[by - 1])
            total = total + self.boxes[4][by - 1].astype(F32)
        self.sums[y, :, 0, :, SIDE] = total.astype(BF16)
        for by in NEAR:
            self.start(
                77 + by - 1,
                self.sums.at[y, self.here.step("x", by), 0, :, SIDE],
                self.boxes[5].at[by - 1],
                self.here.beside("x", by),
            )

    def side_total(self):
        total = self.sums[self.here.pos["y"], self.here.pos["x"], 0, :, SIDE].astype(F32)
        for by in (1, 3, 2):
            self.came(77 + by - 1, self.boxes[5].at[by - 1])
            total = total + self.boxes[5][by - 1].astype(F32)
        return total

    def total(self):
        total = self.sums[self.own(0)].astype(F32)
        for by in (4, 3, 5, 2, 6, 1, 7):
            self.came(60 + by - 1, self.boxes[2].at[by - 1])
            total = total + self.boxes[2][by - 1].astype(F32)
        return total


def kernel(
    tokens,
    target,
    master_up,
    master_down,
    tangent_up,
    tangent_down,
    tokens_out,
    residuals_out,
    both_t,
    grads_t,
    v_master_up,
    v_master_down,
    v_tangent_up,
    v_tangent_down,
    group,
    folded,
    all_tokens,
    weights_up,
    weights_down,
    acc,
    both,
    slopes_ref,
    bend_ref,
    outgoing,
    incoming,
    sums,
    residuals,
    *rest,
):
    boxes = rest[:6]
    in_sems, out_sems, pair_send, pair_recv, group_send, group_recv = rest[6:12]
    first_send, first_recv, scatter_send, scatter_recv, second_send, second_recv = rest[12:]

    here = Here()
    core, pos, me = here.core, here.pos, here.me
    sent = []

    loads = []
    pairs = (
        (master_up, v_master_up),
        (tangent_up, v_tangent_up),
        (master_down, v_master_down),
        (tangent_down, v_tangent_down),
    )
    for number, (source, into) in enumerate(pairs):
        made = pltpu.make_async_copy(source, into, in_sems.at[number])
        made.start()
        loads.append(made)

    barrier = pltpu.get_barrier_semaphore()
    peers = [here.member(by) for by in range(1, GROUP)]
    peers += [here.beside("x", by) for by in range(1, 4)]
    peers += [here.beside("z", by) for by in range(1, 8)]
    for peer in peers:
        pl.semaphore_signal(barrier, inc=1, device_id=peer, device_id_type=MESH)

    def fold(rows):
        rows = rows.astype(F32)
        pieces = [rows[:, k * WIDE : (k + 1) * WIDE] for k in range(GROUP)]
        return jnp.concatenate(pieces, axis=0).astype(BF16)

    folded[core, pos["y"], pos["x"], 0] = fold(tokens[...])
    group[me] = fold(target[...])

    loads[0].wait()
    loads[1].wait()
    zeros_up = jnp.zeros((PAD - HID, 768), BF16)
    for k in range(4):
        columns = slice(k * 768, (k + 1) * 768)
        weights_up[k, 0:HID] = v_master_up[:, columns].astype(BF16)
        weights_up[k, HID:PAD] = zeros_up
        weights_up[k, PAD : PAD + HID] = v_tangent_up[:, columns]
        weights_up[k, PAD + HID :] = zeros_up
    pl.semaphore_wait(barrier, len(peers))

    first = gather(folded, here, PAIRS, first_send, first_recv, sent)
    next(first)

    def group_copy(by, spot):
        return pltpu.make_async_remote_copy(
            src_ref=group.at[spot],
            dst_ref=group.at[spot],
            send_sem=group_send.at[by],
            recv_sem=group_recv.at[by],
            device_id=here.member(by),
            device_id_type=MESH,
        )

    for by in range(1, GROUP):
        made = group_copy(by, me)
        made.start()
        sent.append(made)

    loads[2].wait()
    loads[3].wait()
    zeros_low = jnp.zeros((PAD - HID, 2 * WIDE), BF16)
    zeros_half = jnp.zeros((HID, WIDE), BF16)
    for spot in range(GROUP):
        columns = slice(spot * WIDE, (spot + 1) * WIDE)
        weight = v_master_down[:, columns].astype(BF16)
        weights_down[spot, 0:HID, 0:WIDE] = weight
        weights_down[spot, 0:HID, WIDE:] = v_tangent_down[:, columns]
        weights_down[spot, HID:PAD] = zeros_low
        weights_down[spot, PAD : PAD + HID, 0:WIDE] = zeros_half
        weights_down[spot, PAD : PAD + HID, WIDE:] = weight
        weights_down[spot, PAD + HID :] = zeros_low

    for _ in first:
        pass

    row = lax.broadcasted_iota(jnp.int32, (128, 128), 0)
    column = lax.broadcasted_iota(jnp.int32, (128, 128), 1)
    token = lax.rem(row, 16)
    pick = column == lax.div(token, 2) * 16 + lax.div(row, 16) * 2 + lax.rem(token, 2)
    pick = pick.astype(F32).astype(BF16)

    @pl.loop(0, 4)
    def _(x):
        for z in range(8):
            blocks = folded[:, :, x, z].reshape(128, WIDE)
            rows = jnp.dot(pick, blocks, preferred_element_type=F32).astype(BF16)
            all_tokens[:, x, z] = rows.reshape(GROUP, 16, WIDE)

    stores = [pltpu.make_async_copy(all_tokens, tokens_out, out_sems.at[0])]
    stores[0].start()

    acc[...] = jnp.zeros_like(acc)

    @pl.loop(0, 4)
    def _(k):
        blocks = [all_tokens[2 * k + lower].reshape(TOKENS, WIDE) for lower in range(2)]
        acc[...] += lax.dot_general(
            jnp.concatenate(blocks, axis=1),
            weights_up[k],
            (((1,), (1,)), ((), ())),
            preferred_element_type=F32,
        )

    @pl.loop(0, 4)
    def _(x):
        span = pl.ds(pl.multiple_of(x * 128, 128), 128)
        pre_tangent = acc[span, PAD:]
        activated, slopes, bending = gelu_parts(acc[span, :PAD])
        slopes_ref[span] = slopes
        bend_ref[span] = bending * pre_tangent
        pair = jnp.concatenate([activated, slopes * pre_tangent], axis=1)
        both[x] = pair.astype(BF16).reshape(8, 16, 2 * PAD)

    def pair_copy(far, by):
        return pltpu.make_async_remote_copy(
            src_ref=outgoing.at[far, by],
            dst_ref=incoming.at[far, by],
            send_sem=pair_send.at[far, by],
            recv_sem=pair_recv.at[far, by],
            device_id=here.sibling,
            device_id_type=MESH,
        )

    turns = (1, 3, 2, 0)
    shape = (4, 4, 16, 2 * WIDE)

    def product(far, spot):
        left = both[:, 4 * far : 4 * far + 4].reshape(TOKENS // 2, 2 * PAD)
        return jnp.dot(left, weights_down[spot], preferred_element_type=F32)

    for far in (1, 0):
        for by in turns:
            spot = (1 - core) * 4 + here.step("y", by)
            outgoing[far, by] = product(far, spot).astype(BF16).reshape(shape)
            made = pair_copy(far, by)
            made.start()
            sent.append(made)

    scatter = Scatter(sums, boxes, here, scatter_send, scatter_recv, sent)
    for far in (1, 0):
        for by in turns:
            pair_copy(far, by).wait_recv()
            y = here.step("y", by)
            block = product(far, core * 4 + y)
            block = block + incoming[far, by].astype(F32).reshape(TOKENS // 2, 2 * WIDE)
            sums[y, :, 4 * far : 4 * far + 4] = block.astype(BF16).reshape(shape)
            for to in NEAR:
                scatter.first_x(2 * far, to, by)
            if by:
                scatter.first_y(2 * far + 1, by)
        scatter.side_z(*((4, 3, 5, 2) if far else (6, 1, 7)))

    both_t[...] = both[...].reshape(TOKENS, 2 * PAD).astype(F32).T.astype(BF16)
    for by in turns:
        for q in (2, 3):
            scatter.second(q, by, by == turns[0])
    scatter.third(4, 3, 5, 2)
    for by in turns:
        for q in (1, 0):
            scatter.second(q, by, by == turns[0])
            if by == 0:
                scatter.third(*((6, 7) if q else (1,)))
        if by == 3:
            scatter.side_y()
    scatter.side_x()
    total = scatter.total()
    total = jnp.concatenate([total, scatter.side_total()], axis=1)

    for by in range(1, GROUP):
        group_copy(by, lax.rem(me + GROUP - by, GROUP)).wait_recv()
    row = lax.broadcasted_iota(jnp.int32, (16, 128), 0)
    column = lax.broadcasted_iota(jnp.int32, (16, 128), 1)
    pick = (column == lax.div(row, 2) * 16 + me * 2 + lax.rem(row, 2)).astype(F32).astype(BF16)
    goal = jnp.dot(pick, group[...].reshape(128, WIDE), preferred_element_type=F32)
    pair = jnp.concatenate([total[:, WIDE:], total[:, :WIDE] - goal], axis=1)
    residuals[core, pos["y"], pos["x"], 0] = pair.astype(BF16)

    def keep(number, core):
        row, rows, columns = 0, 8, SIDE
        if number is not None:
            row, rows, columns = PAIRS[number][1], 2, pl.ds(0, MAIN)
        made = pltpu.make_async_copy(
            residuals.at[core, :, :, row : row + rows, :, columns],
            residuals_out.at[core, :, :, row : row + rows, :, columns],
            out_sems.at[len(stores)],
        )
        made.start()
        stores.append(made)

    earlier = list(sent)
    sent.clear()
    last = gather(residuals, here, SETS, second_send, second_recv, sent, keep)
    next(last)
    for made in earlier:
        made.wait_send()
    for _ in last:
        pass

    acc[...] = jnp.zeros_like(acc)

    @pl.loop(0, GROUP)
    def _(spot):
        acc[...] += lax.dot_general(
            residuals[lax.div(spot, 4), lax.rem(spot, 4)].reshape(TOKENS, 2 * WIDE),
            weights_down[spot],
            (((1,), (1,)), ((), ())),
            preferred_element_type=F32,
        )

    for k in range(4):
        span = slice(k * 128, (k + 1) * 128)
        back_dot, back_grad = acc[span, :PAD], acc[span, PAD:]
        slopes = slopes_ref[span]
        grad_pre = (back_grad * slopes).T.astype(BF16)
        grad_pre_dot = (back_dot * slopes + back_grad * bend_ref[span]).T.astype(BF16)
        grads_t[0:PAD, span] = grad_pre
        grads_t[PAD:, span] = grad_pre_dot

    for made in stores:
        made.wait()
    for made in sent:
        made.wait_send()


def update(
    grads_t,
    both_t,
    tokens,
    residuals,
    tangent_up,
    tangent_down,
    moment_up,
    moment_down,
    curve_up,
    curve_down,
    step_up,
    step_down,
    moment_up_next,
    moment_down_next,
    curve_up_next,
    curve_down_next,
):
    loss_scale = 1.0 / math.sqrt(TOKENS)
    wide = [tokens[k].reshape(TOKENS, WIDE) for k in range(2)]
    up = jnp.dot(grads_t[...], jnp.concatenate(wide, axis=1), preferred_element_type=F32)
    step_up[...], moment_up_next[...], curve_up_next[...] = refresh(
        moment_up[...],
        curve_up[...],
        loss_scale * up[:HID],
        loss_scale * up[PAD : PAD + HID],
        tangent_up[...],
    )
    grad, hvp = [], []
    for k in range(2):
        down = jnp.dot(
            both_t[...],
            residuals[k].reshape(TOKENS, 2 * WIDE),
            preferred_element_type=F32,
        )
        grad.append(down[:HID, WIDE:])
        hvp.append(down[:HID, :WIDE] + down[PAD : PAD + HID, WIDE:])
    step_down[...], moment_down_next[...], curve_down_next[...] = refresh(
        moment_down[...],
        curve_down[...],
        loss_scale * jnp.concatenate(grad, axis=1),
        loss_scale * jnp.concatenate(hvp, axis=1),
        tangent_down[...],
    )


def per_device(
    tokens,
    target,
    master_up,
    master_down,
    tangent_up,
    tangent_down,
    moment_up,
    moment_down,
    curve_up,
    curve_down,
):
    wide32 = jax.ShapeDtypeStruct((HID, D), F32)
    wide16 = jax.ShapeDtypeStruct((HID, D), BF16)
    blocks = (4, 4, 8, 16)
    any_spec = pl.BlockSpec(memory_space=pl.ANY)
    vmem_spec = pl.BlockSpec(memory_space=pltpu.VMEM)
    scratch = [pltpu.VMEM((HID, D), F32)] * 2 + [pltpu.VMEM((HID, D), BF16)] * 2
    scratch += [
        pltpu.VMEM((GROUP, 16, WIDE), BF16),
        pltpu.VMEM((2,) + blocks + (WIDE,), BF16),
        pltpu.VMEM((GROUP, 4, 8, 16, WIDE), BF16),
        pltpu.VMEM((4, 2 * PAD, 768), BF16),
        pltpu.VMEM((GROUP, 2 * PAD, 2 * WIDE), BF16),
        pltpu.VMEM((TOKENS, 2 * PAD), F32),
        pltpu.VMEM((4, 8, 16, 2 * PAD), BF16),
        pltpu.VMEM((TOKENS, PAD), F32),
        pltpu.VMEM((TOKENS, PAD), F32),
        pltpu.VMEM((2, 4, 4, 4, 16, 2 * WIDE), BF16),
        pltpu.VMEM((2, 4, 4, 4, 16, 2 * WIDE), BF16),
        pltpu.VMEM(blocks + (2 * WIDE,), BF16),
        pltpu.VMEM((2,) + blocks + (2 * WIDE,), BF16),
        pltpu.VMEM((3, 4, 8, 16, MAIN), BF16),
        pltpu.VMEM((3, 8, 16, MAIN), BF16),
        pltpu.VMEM((7, 16, MAIN), BF16),
        pltpu.VMEM((7, 4, 4, 16, 2 * WIDE - MAIN), BF16),
        pltpu.VMEM((3, 4, 16, 2 * WIDE - MAIN), BF16),
        pltpu.VMEM((3, 16, 2 * WIDE - MAIN), BF16),
    ]
    dma = pltpu.SemaphoreType.DMA
    scratch += [
        dma((4,)),
        dma((11,)),
        dma((2, 4)),
        dma((2, 4)),
        dma((GROUP,)),
        dma((GROUP,)),
        dma((GATHER_COUNT,)),
        dma((GATHER_COUNT,)),
        dma((SCATTER_COUNT,)),
        dma((SCATTER_COUNT,)),
        dma((GATHER_COUNT,)),
        dma((GATHER_COUNT,)),
    ]
    all_tokens, residuals, both_t, grads_t = pl.pallas_call(
        kernel,
        out_shape=(
            jax.ShapeDtypeStruct((GROUP, 4, 8, 16, WIDE), BF16),
            jax.ShapeDtypeStruct((2,) + blocks + (2 * WIDE,), BF16),
            jax.ShapeDtypeStruct((2 * PAD, TOKENS), BF16),
            jax.ShapeDtypeStruct((2 * PAD, TOKENS), BF16),
        ),
        in_specs=[vmem_spec] * 2 + [any_spec] * 4,
        out_specs=(any_spec, any_spec, vmem_spec, vmem_spec),
        scratch_shapes=scratch,
        compiler_params=pltpu.CompilerParams(
            collective_id=0, has_side_effects=True, vmem_limit_bytes=62 * 1024 * 1024
        ),
        cost_estimate=pl.CostEstimate(
            flops=3_000_000_000, bytes_accessed=16_000_000, transcendentals=131072
        ),
    )(tokens, target, master_up, master_down, tangent_up, tangent_down)
    residuals = residuals.reshape((GROUP, 4, 8, 16, 2 * WIDE))
    whole = pl.BlockSpec((2 * PAD, TOKENS), lambda spot: (0, 0))
    part = pl.BlockSpec((HID, 2 * WIDE), lambda spot: (0, spot))
    return pl.pallas_call(
        update,
        grid=(GROUP // 2,),
        out_shape=(wide32, wide32, wide16, wide16, wide16, wide16),
        in_specs=[
            whole,
            whole,
            pl.BlockSpec((2, 4, 8, 16, WIDE), lambda spot: (spot, 0, 0, 0, 0)),
            pl.BlockSpec((2, 4, 8, 16, 2 * WIDE), lambda spot: (spot, 0, 0, 0, 0)),
        ]
        + [part] * 6,
        out_specs=(part,) * 6,
        compiler_params=pltpu.CompilerParams(vmem_limit_bytes=62 * 1024 * 1024),
        cost_estimate=pl.CostEstimate(
            flops=1_500_000_000, bytes_accessed=18_000_000, transcendentals=0
        ),
    )(
        grads_t,
        both_t,
        all_tokens,
        residuals,
        tangent_up,
        tangent_down,
        moment_up,
        moment_down,
        curve_up,
        curve_down,
    )


def solution(mesh):
    rows = P(("dp", "tensor"), None)
    return jax.shard_map(
        per_device, mesh=mesh, in_specs=(rows,) * 10, out_specs=(rows,) * 6, check_vma=False
    )
```

```python
import math

import jax
import jax.numpy as jnp
from jax import lax
from jax.experimental import pallas as pl
from jax.experimental.pallas import tpu as pltpu
from jax.sharding import PartitionSpec as P

TOKENS = 512
D = 3072
HID = 96
PAD = 128
PARTS = 3
SIZE = {"y": 4, "x": 4, "z": 8}
AXES = ("y", "x", "z")
GROUP = 8
WIDE = D // GROUP
NEAR = (2, 1, 3)
PARTS = (("y", "x"), ("x", "y"))
OFFSETS = (0, 1, 7, 6, 2, 3, 5, 4)
PAIRS = ((0, 0, 2), (1, 2, 2), (0, 4, 2), (1, 6, 2))
SETS = ((0, 0, 1), (0, 1, 1), (1, 2, 1), (1, 3, 1), (0, 4, 2), (1, 6, 2))
MAIN = 640
SIDE = pl.ds(MAIN, 2 * WIDE - MAIN)
GATHER_COUNT = 7 + 6 * 15 + 4 + 1 + 3 + 3 + 7
SCATTER_COUNT = 4 * 15 + 7 + 7 + 3 + 3

beta_first = 0.965
beta_second = 0.99
gamma_scale = 0.01
ratio_floor = 0.01
root_half = 0.7071067811865476
inv_root_tau = 0.3989422804014327

F32 = jnp.float32
BF16 = jnp.bfloat16
MESH = pl.DeviceIdType.MESH


def gelu_parts(pre_act):
    normal_cdf = 0.5 * (1.0 + lax.erf(pre_act * root_half))
    density = jnp.exp(-0.5 * pre_act * pre_act) * inv_root_tau
    return (
        pre_act * normal_cdf,
        normal_cdf + pre_act * density,
        density * (2.0 - pre_act * pre_act),
    )


def refresh(moment, curve, grad, hvp, tangent):
    moment_f = beta_first * moment.astype(F32) + (1.0 - beta_first) * grad
    curve_f = beta_second * curve.astype(F32) + (1.0 - beta_second) * tangent.astype(F32) * hvp
    step = jnp.clip(moment_f / jnp.maximum(gamma_scale * curve_f, ratio_floor), -1.0, 1.0)
    return step, moment_f.astype(BF16), curve_f.astype(BF16)


def wrap(value, size):
    return lax.rem(value + size, size)


class Here:
    def __init__(self):
        dp = lax.axis_index("dp")
        tensor = lax.axis_index("tensor")
        self.core = lax.rem(tensor, 2)
        self.pos = {
            "x": lax.rem(lax.div(dp, 8), 4),
            "z": lax.rem(dp, 8),
            "y": lax.div(tensor, 2) * 2 + lax.div(dp, 32),
        }
        self.me = self.core * 4 + self.pos["y"]
        self.steps = {
            (axis, by): wrap(self.pos[axis] + by, SIZE[axis])
            for axis in AXES
            for by in range(SIZE[axis])
        }
        self.devices = {
            key: self.device({**self.pos, key[0]: spot}, self.core)
            for key, spot in self.steps.items()
            if key[1]
        }
        self.sibling = self.device(self.pos, 1 - self.core)

    def device(self, pos, core):
        y = pos["y"]
        return (
            lax.rem(y, 2) * 32 + pos["x"] * 8 + pos["z"],
            lax.div(y, 2) * 2 + core,
        )

    def member(self, by):
        spot = lax.rem(self.me + by, GROUP)
        return self.device({**self.pos, "y": lax.rem(spot, 4)}, lax.div(spot, 4))

    def step(self, axis, by):
        return self.steps[(axis, by % SIZE[axis])]

    def beside(self, axis, by):
        return self.devices[(axis, by)]


def place(where):
    return tuple(where[axis] for axis in AXES)


def gather(buffer, here, sets, send_sems, recv_sems, sent, keep=None):
    side = keep is not None
    columns = pl.ds(0, MAIN if side else WIDE)
    mine = buffer.at[here.core]
    other = buffer.at[1 - here.core]

    def copy(index, source, into, target):
        return pltpu.make_async_remote_copy(
            src_ref=source,
            dst_ref=into,
            send_sem=send_sems.at[index],
            recv_sem=recv_sems.at[index],
            device_id=target,
            device_id_type=MESH,
        )

    def start(index, source, into, target):
        made = copy(index, source, into, target)
        made.start()
        sent.append(made)

    def set_block(q, m, f):
        part, row, rows = sets[q]
        middle, final = PARTS[part]
        where = {
            middle: here.step(middle, -m),
            final: here.step(final, -f),
            "z": pl.ds(row, rows),
        }
        return mine.at[place(where) + (slice(None), columns)]

    def launch(q):
        middle, final = PARTS[sets[q][0]]
        own = set_block(q, 0, 0)
        for m in NEAR:
            start(7 + q * 15 + m - 1, own, own, here.beside(middle, m))
        for f in NEAR:
            start(10 + q * 15 + f - 1, own, own, here.beside(final, f))

    def arrive(*offsets):
        for offset in offsets:
            where = place({**here.pos, "z": OFFSETS.index(offset)})
            came = mine.at[where + (slice(None), columns)]
            copy(7 - offset, came, came, here.sibling).wait_recv()

    def forward(q):
        final = PARTS[sets[q][0]][1]
        for m in (1, 3, 2):
            came = set_block(q, m, 0)
            copy(7 + q * 15 + m - 1, came, came, here.sibling).wait_recv()
            for f in NEAR:
                start(13 + q * 15 + (m - 1) * 3 + f - 1, came, came, here.beside(final, f))

    def finish(q):
        for m in (0, 1, 3, 2):
            for f in (1, 3, 2):
                index = (10 if m == 0 else 13 + (m - 1) * 3) + q * 15 + f - 1
                came = set_block(q, m, f)
                copy(index, came, came, here.sibling).wait_recv()

    def hand_on(number):
        row = PAIRS[number][1]
        ref = mine.at[:, :, row : row + 2, :, columns]
        start(97 + number, ref, ref, here.sibling)

    here_y, here_x = here.pos["y"], here.pos["x"]

    def side_x():
        ref = mine.at[here_y, here_x, 0, :, SIDE]
        for by in NEAR:
            start(102 + by - 1, ref, ref, here.beside("x", by))

    def side_y():
        for by in NEAR:
            ref = mine.at[here_y, here.step("x", -by), 0, :, SIDE]
            copy(102 + by - 1, ref, ref, here.sibling).wait_recv()
        ref = mine.at[here_y, :, 0, :, SIDE]
        for by in NEAR:
            start(105 + by - 1, ref, ref, here.beside("y", by))

    def side_z():
        for by in NEAR:
            ref = mine.at[here.step("y", -by), :, 0, :, SIDE]
            copy(105 + by - 1, ref, ref, here.sibling).wait_recv()
        for by in (4, 3, 5, 2, 6, 1, 7):
            into = mine.at[:, :, OFFSETS.index(8 - by), :, SIDE]
            start(108 + by - 1, mine.at[:, :, 0, :, SIDE], into, here.beside("z", by))

    def side_end():
        for by in (1, 7, 2, 6, 3, 5, 4):
            ref = mine.at[:, :, OFFSETS.index(8 - by), :, SIDE]
            copy(108 + by - 1, ref, ref, here.sibling).wait_recv()
        ref = mine.at[:, :, :, :, SIDE]
        start(101, ref, ref, here.sibling)
        keep(None, here.core)

    if side:
        side_x()
    own = mine.at[place({**here.pos, "z": 0}) + (slice(None), columns)]
    for by in (1, 7, 2, 6, 3, 5, 4):
        into = mine.at[place({**here.pos, "z": OFFSETS.index(8 - by)}) + (slice(None), columns)]
        start(by - 1, own, into, here.beside("z", by))
    if len(sets) == 6:
        launch(0)
        yield
        arrive(1)
        launch(1)
        side_y()
        arrive(7)
        launch(2)
        arrive(6)
        launch(3)
        forward(0)
        side_z()
        arrive(2, 3)
        launch(4)
        arrive(5, 4)
        launch(5)
        for q in (1, 2, 3, 4, 5):
            forward(q)
        completing = (1, 3, 4, 5)
    else:
        yield
        arrive(1)
        launch(0)
        arrive(7, 6)
        launch(1)
        arrive(2, 3)
        launch(2)
        arrive(5, 4)
        launch(3)
        for q in range(4):
            forward(q)
        completing = (0, 1, 2, 3)
    for q in range(len(sets)):
        finish(q)
        if side and q == 3:
            side_end()
        if q in completing:
            hand_on(completing.index(q))
            if keep is not None:
                keep(completing.index(q), here.core)
    for number, (_, row, rows) in enumerate(PAIRS):
        came = other.at[:, :, row : row + rows, :, columns]
        copy(97 + number, came, came, here.sibling).wait_recv()
        if keep is not None:
            keep(number, 1 - here.core)
    if side:
        came = other.at[:, :, :, :, SIDE]
        copy(101, came, came, here.sibling).wait_recv()
        keep(None, 1 - here.core)


class Scatter:
    def __init__(self, sums, boxes, here, send_sems, recv_sems, sent):
        self.sums, self.boxes, self.here = sums, boxes, here
        self.send_sems, self.recv_sems, self.sent = send_sems, recv_sems, sent

    def copy(self, index, source, into, target):
        return pltpu.make_async_remote_copy(
            src_ref=source,
            dst_ref=into,
            send_sem=self.send_sems.at[index],
            recv_sem=self.recv_sems.at[index],
            device_id=target,
            device_id_type=MESH,
        )

    def start(self, *what):
        made = self.copy(*what)
        made.start()
        self.sent.append(made)

    def rows(self, q):
        return pl.ds(PAIRS[q][1], PAIRS[q][2])

    def piece(self, q, by_first, by_second):
        second, first = PARTS[PAIRS[q][0]]
        where = {
            first: self.here.step(first, by_first),
            second: self.here.step(second, by_second),
            "z": self.rows(q),
        }
        return place(where) + (slice(None), pl.ds(0, MAIN))

    def first_x(self, q, by, by_second):
        self.start(
            q * 15 + (by - 1) * 4 + by_second,
            self.sums.at[self.piece(q, by, by_second)],
            self.boxes[0].at[by - 1, by_second, self.rows(q)],
            self.here.beside("x", by),
        )

    def first_y(self, q, by):
        self.start(
            q * 15 + by - 1,
            self.sums.at[self.here.step("y", by), :, self.rows(q), :, pl.ds(0, MAIN)],
            self.boxes[0].at[by - 1, :, self.rows(q)],
            self.here.beside("y", by),
        )

    def came(self, index, into):
        self.copy(index, into, into, self.here.sibling).wait_recv()

    def second(self, q, by_second, fresh):
        where = self.piece(q, 0, by_second)
        total = self.sums[where].astype(F32)
        rows = self.rows(q)
        for by in (1, 3, 2):
            if PAIRS[q][0] == 0:
                into = (by - 1, by_second, rows)
                self.came(q * 15 + (by - 1) * 4 + by_second, self.boxes[0].at[into])
            else:
                into = (by - 1, self.here.step("x", by_second), rows)
                if fresh:
                    self.came(q * 15 + by - 1, self.boxes[0].at[by - 1, :, rows])
            total = total + self.boxes[0][into].astype(F32)
        if by_second:
            self.sums[where] = total.astype(BF16)
            self.start(
                q * 15 + 12 + by_second - 1,
                self.sums.at[where],
                self.boxes[1].at[by_second - 1, rows],
                self.here.beside(PARTS[PAIRS[q][0]][0], by_second),
            )
            return
        for by in (1, 3, 2):
            into = (by - 1, rows)
            self.came(q * 15 + 12 + by - 1, self.boxes[1].at[into])
            total = total + self.boxes[1][into].astype(F32)
        self.sums[where] = total.astype(BF16)

    def third(self, *offsets):
        for by in offsets:
            self.start(
                60 + by - 1,
                self.sums.at[self.own(OFFSETS.index(by))],
                self.boxes[2].at[by - 1],
                self.here.beside("z", by),
            )

    def own(self, row):
        return place({**self.here.pos, "z": row}) + (slice(None), pl.ds(0, MAIN))

    def side_z(self, *offsets):
        for by in offsets:
            self.start(
                67 + by - 1,
                self.sums.at[:, :, OFFSETS.index(by), :, SIDE],
                self.boxes[3].at[by - 1],
                self.here.beside("z", by),
            )

    def side_y(self):
        total = self.sums[:, :, 0, :, SIDE].astype(F32)
        for by in (1, 7, 2, 6, 3, 5, 4):
            self.came(67 + by - 1, self.boxes[3].at[by - 1])
            total = total + self.boxes[3][by - 1].astype(F32)
        self.sums[:, :, 0, :, SIDE] = total.astype(BF16)
        for by in NEAR:
            self.start(
                74 + by - 1,
                self.sums.at[self.here.step("y", by), :, 0, :, SIDE],
                self.boxes[4].at[by - 1],
                self.here.beside("y", by),
            )

    def side_x(self):
        y = self.here.pos["y"]
        total = self.sums[y, :, 0, :, SIDE].astype(F32)
        for by in (1, 3, 2):
            self.came(74 + by - 1, self.boxes[4].at[by - 1])
            total = total + self.boxes[4][by - 1].astype(F32)
        self.sums[y, :, 0, :, SIDE] = total.astype(BF16)
        for by in NEAR:
            self.start(
                77 + by - 1,
                self.sums.at[y, self.here.step("x", by), 0, :, SIDE],
                self.boxes[5].at[by - 1],
                self.here.beside("x", by),
            )

    def side_total(self):
        total = self.sums[self.here.pos["y"], self.here.pos["x"], 0, :, SIDE].astype(F32)
        for by in (1, 3, 2):
            self.came(77 + by - 1, self.boxes[5].at[by - 1])
            total = total + self.boxes[5][by - 1].astype(F32)
        return total

    def total(self):
        total = self.sums[self.own(0)].astype(F32)
        for by in (4, 3, 5, 2, 6, 1, 7):
            self.came(60 + by - 1, self.boxes[2].at[by - 1])
            total = total + self.boxes[2][by - 1].astype(F32)
        return total


def kernel(
    tokens,
    target,
    master_up,
    master_down,
    tangent_up,
    tangent_down,
    tokens_out,
    residuals_out,
    both_t,
    grads_t,
    v_master_up,
    v_master_down,
    v_tangent_up,
    v_tangent_down,
    group,
    folded,
    all_tokens,
    weights_up,
    weights_down,
    acc,
    both,
    slopes_ref,
    bend_ref,
    outgoing,
    incoming,
    sums,
    residuals,
    *rest,
):
    boxes = rest[:6]
    in_sems, out_sems, pair_send, pair_recv, group_send, group_recv = rest[6:12]
    first_send, first_recv, scatter_send, scatter_recv, second_send, second_recv = rest[12:]

    here = Here()
    core, pos, me = here.core, here.pos, here.me
    sent = []

    loads = []
    pairs = (
        (master_up, v_master_up),
        (tangent_up, v_tangent_up),
        (master_down, v_master_down),
        (tangent_down, v_tangent_down),
    )
    for number, (source, into) in enumerate(pairs):
        made = pltpu.make_async_copy(source, into, in_sems.at[number])
        made.start()
        loads.append(made)

    barrier = pltpu.get_barrier_semaphore()
    peers = [here.member(by) for by in range(1, GROUP)]
    peers += [here.beside("x", by) for by in range(1, 4)]
    peers += [here.beside("z", by) for by in range(1, 8)]
    for peer in peers:
        pl.semaphore_signal(barrier, inc=1, device_id=peer, device_id_type=MESH)

    def fold(rows):
        rows = rows.astype(F32)
        pieces = [rows[:, k * WIDE : (k + 1) * WIDE] for k in range(GROUP)]
        return jnp.concatenate(pieces, axis=0).astype(BF16)

    folded[core, pos["y"], pos["x"], 0] = fold(tokens[...])
    group[me] = fold(target[...])

    loads[0].wait()
    loads[1].wait()
    zeros_up = jnp.zeros((PAD - HID, 768), BF16)
    for k in range(4):
        columns = slice(k * 768, (k + 1) * 768)
        weights_up[k, 0:HID] = v_master_up[:, columns].astype(BF16)
        weights_up[k, HID:PAD] = zeros_up
        weights_up[k, PAD : PAD + HID] = v_tangent_up[:, columns]
        weights_up[k, PAD + HID :] = zeros_up
    pl.semaphore_wait(barrier, len(peers))

    first = gather(folded, here, PAIRS, first_send, first_recv, sent)
    next(first)

    def group_copy(by, spot):
        return pltpu.make_async_remote_copy(
            src_ref=group.at[spot],
            dst_ref=group.at[spot],
            send_sem=group_send.at[by],
            recv_sem=group_recv.at[by],
            device_id=here.member(by),
            device_id_type=MESH,
        )

    for by in range(1, GROUP):
        made = group_copy(by, me)
        made.start()
        sent.append(made)

    loads[2].wait()
    loads[3].wait()
    zeros_low = jnp.zeros((PAD - HID, 2 * WIDE), BF16)
    zeros_half = jnp.zeros((HID, WIDE), BF16)
    for spot in range(GROUP):
        columns = slice(spot * WIDE, (spot + 1) * WIDE)
        weight = v_master_down[:, columns].astype(BF16)
        weights_down[spot, 0:HID, 0:WIDE] = weight
        weights_down[spot, 0:HID, WIDE:] = v_tangent_down[:, columns]
        weights_down[spot, HID:PAD] = zeros_low
        weights_down[spot, PAD : PAD + HID, 0:WIDE] = zeros_half
        weights_down[spot, PAD : PAD + HID, WIDE:] = weight
        weights_down[spot, PAD + HID :] = zeros_low

    for _ in first:
        pass

    row = lax.broadcasted_iota(jnp.int32, (128, 128), 0)
    column = lax.broadcasted_iota(jnp.int32, (128, 128), 1)
    token = lax.rem(row, 16)
    pick = column == lax.div(token, 2) * 16 + lax.div(row, 16) * 2 + lax.rem(token, 2)
    pick = pick.astype(F32).astype(BF16)

    @pl.loop(0, 4)
    def _(x):
        for z in range(8):
            blocks = folded[:, :, x, z].reshape(128, WIDE)
            rows = jnp.dot(pick, blocks, preferred_element_type=F32).astype(BF16)
            all_tokens[:, x, z] = rows.reshape(GROUP, 16, WIDE)

    stores = [pltpu.make_async_copy(all_tokens, tokens_out, out_sems.at[0])]
    stores[0].start()

    acc[...] = jnp.zeros_like(acc)

    @pl.loop(0, 4)
    def _(k):
        blocks = [all_tokens[2 * k + lower].reshape(TOKENS, WIDE) for lower in range(2)]
        acc[...] += lax.dot_general(
            jnp.concatenate(blocks, axis=1),
            weights_up[k],
            (((1,), (1,)), ((), ())),
            preferred_element_type=F32,
        )

    @pl.loop(0, 4)
    def _(x):
        span = pl.ds(pl.multiple_of(x * 128, 128), 128)
        pre_tangent = acc[span, PAD:]
        activated, slopes, bending = gelu_parts(acc[span, :PAD])
        slopes_ref[span] = slopes
        bend_ref[span] = bending * pre_tangent
        pair = jnp.concatenate([activated, slopes * pre_tangent], axis=1)
        both[x] = pair.astype(BF16).reshape(8, 16, 2 * PAD)

    def pair_copy(far, by):
        return pltpu.make_async_remote_copy(
            src_ref=outgoing.at[far, by],
            dst_ref=incoming.at[far, by],
            send_sem=pair_send.at[far, by],
            recv_sem=pair_recv.at[far, by],
            device_id=here.sibling,
            device_id_type=MESH,
        )

    turns = (1, 3, 2, 0)
    shape = (4, 4, 16, 2 * WIDE)

    def product(far, spot):
        left = both[:, 4 * far : 4 * far + 4].reshape(TOKENS // 2, 2 * PAD)
        return jnp.dot(left, weights_down[spot], preferred_element_type=F32)

    for far in (1, 0):
        for by in turns:
            spot = (1 - core) * 4 + here.step("y", by)
            outgoing[far, by] = product(far, spot).astype(BF16).reshape(shape)
            made = pair_copy(far, by)
            made.start()
            sent.append(made)

    scatter = Scatter(sums, boxes, here, scatter_send, scatter_recv, sent)
    for far in (1, 0):
        for by in turns:
            pair_copy(far, by).wait_recv()
            y = here.step("y", by)
            block = product(far, core * 4 + y)
            block = block + incoming[far, by].astype(F32).reshape(TOKENS // 2, 2 * WIDE)
            sums[y, :, 4 * far : 4 * far + 4] = block.astype(BF16).reshape(shape)
            for to in NEAR:
                scatter.first_x(2 * far, to, by)
            if by:
                scatter.first_y(2 * far + 1, by)
        scatter.side_z(*((4, 3, 5, 2) if far else (6, 1, 7)))

    both_t[...] = both[...].reshape(TOKENS, 2 * PAD).astype(F32).T.astype(BF16)
    for by in turns:
        for q in (2, 3):
            scatter.second(q, by, by == turns[0])
    scatter.third(4, 3, 5, 2)
    for by in turns:
        for q in (1, 0):
            scatter.second(q, by, by == turns[0])
            if by == 0:
                scatter.third(*((6, 7) if q else (1,)))
        if by == 3:
            scatter.side_y()
    scatter.side_x()
    total = scatter.total()
    total = jnp.concatenate([total, scatter.side_total()], axis=1)

    for by in range(1, GROUP):
        group_copy(by, lax.rem(me + GROUP - by, GROUP)).wait_recv()
    row = lax.broadcasted_iota(jnp.int32, (16, 128), 0)
    column = lax.broadcasted_iota(jnp.int32, (16, 128), 1)
    pick = (column == lax.div(row, 2) * 16 + me * 2 + lax.rem(row, 2)).astype(F32).astype(BF16)
    goal = jnp.dot(pick, group[...].reshape(128, WIDE), preferred_element_type=F32)
    pair = jnp.concatenate([total[:, WIDE:], total[:, :WIDE] - goal], axis=1)
    residuals[core, pos["y"], pos["x"], 0] = pair.astype(BF16)

    def keep(number, core):
        row, rows, columns = 0, 8, SIDE
        if number is not None:
            row, rows, columns = PAIRS[number][1], 2, pl.ds(0, MAIN)
        made = pltpu.make_async_copy(
            residuals.at[core, :, :, row : row + rows, :, columns],
            residuals_out.at[core, :, :, row : row + rows, :, columns],
            out_sems.at[len(stores)],
        )
        made.start()
        stores.append(made)

    earlier = list(sent)
    sent.clear()
    last = gather(residuals, here, SETS, second_send, second_recv, sent, keep)
    next(last)
    for made in earlier:
        made.wait_send()
    for _ in last:
        pass

    acc[...] = jnp.zeros_like(acc)

    @pl.loop(0, GROUP)
    def _(spot):
        acc[...] += lax.dot_general(
            residuals[lax.div(spot, 4), lax.rem(spot, 4)].reshape(TOKENS, 2 * WIDE),
            weights_down[spot],
            (((1,), (1,)), ((), ())),
            preferred_element_type=F32,
        )

    for k in range(4):
        span = slice(k * 128, (k + 1) * 128)
        back_dot, back_grad = acc[span, :PAD], acc[span, PAD:]
        slopes = slopes_ref[span]
        grad_pre = (back_grad * slopes).T.astype(BF16)
        grad_pre_dot = (back_dot * slopes + back_grad * bend_ref[span]).T.astype(BF16)
        grads_t[0:PAD, span] = grad_pre
        grads_t[PAD:, span] = grad_pre_dot

    for made in stores:
        made.wait()
    for made in sent:
        made.wait_send()


def update(
    grads_t,
    both_t,
    tokens,
    residuals,
    tangent_up,
    tangent_down,
    moment_up,
    moment_down,
    curve_up,
    curve_down,
    step_up,
    step_down,
    moment_up_next,
    moment_down_next,
    curve_up_next,
    curve_down_next,
):
    first = 2 * pl.program_id(0)
    loss_scale = 1.0 / math.sqrt(TOKENS)
    wide = [tokens[first + k].reshape(TOKENS, WIDE) for k in range(2)]
    up = jnp.dot(grads_t[...], jnp.concatenate(wide, axis=1), preferred_element_type=F32)
    step_up[...], moment_up_next[...], curve_up_next[...] = refresh(
        moment_up[...],
        curve_up[...],
        loss_scale * up[:HID],
        loss_scale * up[PAD : PAD + HID],
        tangent_up[...],
    )
    grad, hvp = [], []
    for k in range(2):
        down = jnp.dot(
            both_t[...],
            residuals[first + k].reshape(TOKENS, 2 * WIDE),
            preferred_element_type=F32,
        )
        grad.append(down[:HID, WIDE:])
        hvp.append(down[:HID, :WIDE] + down[PAD : PAD + HID, WIDE:])
    step_down[...], moment_down_next[...], curve_down_next[...] = refresh(
        moment_down[...],
        curve_down[...],
        loss_scale * jnp.concatenate(grad, axis=1),
        loss_scale * jnp.concatenate(hvp, axis=1),
        tangent_down[...],
    )


def per_device(
    tokens,
    target,
    master_up,
    master_down,
    tangent_up,
    tangent_down,
    moment_up,
    moment_down,
    curve_up,
    curve_down,
):
    wide32 = jax.ShapeDtypeStruct((HID, D), F32)
    wide16 = jax.ShapeDtypeStruct((HID, D), BF16)
    blocks = (4, 4, 8, 16)
    any_spec = pl.BlockSpec(memory_space=pl.ANY)
    vmem_spec = pl.BlockSpec(memory_space=pltpu.VMEM)
    scratch = [pltpu.VMEM((HID, D), F32)] * 2 + [pltpu.VMEM((HID, D), BF16)] * 2
    scratch += [
        pltpu.VMEM((GROUP, 16, WIDE), BF16),
        pltpu.VMEM((2,) + blocks + (WIDE,), BF16),
        pltpu.VMEM((GROUP, 4, 8, 16, WIDE), BF16),
        pltpu.VMEM((4, 2 * PAD, 768), BF16),
        pltpu.VMEM((GROUP, 2 * PAD, 2 * WIDE), BF16),
        pltpu.VMEM((TOKENS, 2 * PAD), F32),
        pltpu.VMEM((4, 8, 16, 2 * PAD), BF16),
        pltpu.VMEM((TOKENS, PAD), F32),
        pltpu.VMEM((TOKENS, PAD), F32),
        pltpu.VMEM((2, 4, 4, 4, 16, 2 * WIDE), BF16),
        pltpu.VMEM((2, 4, 4, 4, 16, 2 * WIDE), BF16),
        pltpu.VMEM(blocks + (2 * WIDE,), BF16),
        pltpu.VMEM((2,) + blocks + (2 * WIDE,), BF16),
        pltpu.VMEM((3, 4, 8, 16, MAIN), BF16),
        pltpu.VMEM((3, 8, 16, MAIN), BF16),
        pltpu.VMEM((7, 16, MAIN), BF16),
        pltpu.VMEM((7, 4, 4, 16, 2 * WIDE - MAIN), BF16),
        pltpu.VMEM((3, 4, 16, 2 * WIDE - MAIN), BF16),
        pltpu.VMEM((3, 16, 2 * WIDE - MAIN), BF16),
    ]
    dma = pltpu.SemaphoreType.DMA
    scratch += [
        dma((4,)),
        dma((11,)),
        dma((2, 4)),
        dma((2, 4)),
        dma((GROUP,)),
        dma((GROUP,)),
        dma((GATHER_COUNT,)),
        dma((GATHER_COUNT,)),
        dma((SCATTER_COUNT,)),
        dma((SCATTER_COUNT,)),
        dma((GATHER_COUNT,)),
        dma((GATHER_COUNT,)),
    ]
    all_tokens, residuals, both_t, grads_t = pl.pallas_call(
        kernel,
        out_shape=(
            pltpu.VMEM((GROUP, 4, 8, 16, WIDE), BF16),
            pltpu.VMEM((2,) + blocks + (2 * WIDE,), BF16),
            pltpu.VMEM((2 * PAD, TOKENS), BF16),
            pltpu.VMEM((2 * PAD, TOKENS), BF16),
        ),
        in_specs=[vmem_spec] * 2 + [any_spec] * 4,
        out_specs=(vmem_spec,) * 4,
        scratch_shapes=scratch,
        compiler_params=pltpu.CompilerParams(
            collective_id=0, has_side_effects=True, vmem_limit_bytes=49 * 1024 * 1024
        ),
        cost_estimate=pl.CostEstimate(
            flops=3_000_000_000, bytes_accessed=16_000_000, transcendentals=131072
        ),
    )(tokens, target, master_up, master_down, tangent_up, tangent_down)
    residuals = residuals.reshape((GROUP, 4, 8, 16, 2 * WIDE))
    whole = pl.BlockSpec((2 * PAD, TOKENS), lambda spot: (0, 0))
    part = pl.BlockSpec((HID, 2 * WIDE), lambda spot: (0, spot))
    return pl.pallas_call(
        update,
        grid=(GROUP // 2,),
        out_shape=(wide32, wide32, wide16, wide16, wide16, wide16),
        in_specs=[
            whole,
            whole,
            vmem_spec,
            vmem_spec,
        ]
        + [part] * 6,
        out_specs=(part,) * 6,
        compiler_params=pltpu.CompilerParams(vmem_limit_bytes=30 * 1024 * 1024),
        cost_estimate=pl.CostEstimate(
            flops=1_500_000_000, bytes_accessed=18_000_000, transcendentals=0
        ),
    )(
        grads_t,
        both_t,
        all_tokens,
        residuals,
        tangent_up,
        tangent_down,
        moment_up,
        moment_down,
        curve_up,
        curve_down,
    )


def solution(mesh):
    rows = P(("dp", "tensor"), None)
    return jax.shard_map(
        per_device, mesh=mesh, in_specs=(rows,) * 10, out_specs=(rows,) * 6, check_vma=False
    )
```

```python
import math

import jax
import jax.numpy as jnp
from jax import lax
from jax.experimental import pallas as pl
from jax.experimental.pallas import tpu as pltpu
from jax.sharding import PartitionSpec as P

TOKENS = 512
D = 3072
HID = 96
PAD = 128
PARTS = 3
SIZE = {"y": 4, "x": 4, "z": 8}
AXES = ("y", "x", "z")
GROUP = 8
WIDE = D // GROUP
NEAR = (2, 1, 3)
PARTS = (("y", "x"), ("x", "y"))
OFFSETS = (0, 1, 7, 6, 2, 3, 5, 4)
PAIRS = ((0, 0, 2), (1, 2, 2), (0, 4, 2), (1, 6, 2))
SETS = ((0, 0, 1), (0, 1, 1), (1, 2, 1), (1, 3, 1), (0, 4, 2), (1, 6, 2))
MAIN = 640
SIDE = pl.ds(MAIN, 2 * WIDE - MAIN)
GATHER_COUNT = 7 + 6 * 15 + 4 + 1 + 3 + 3 + 7
SCATTER_COUNT = 4 * 15 + 7 + 7 + 3 + 3

beta_first = 0.965
beta_second = 0.99
gamma_scale = 0.01
ratio_floor = 0.01
root_half = 0.7071067811865476
inv_root_tau = 0.3989422804014327

F32 = jnp.float32
BF16 = jnp.bfloat16
MESH = pl.DeviceIdType.MESH


def gelu_parts(pre_act):
    normal_cdf = 0.5 * (1.0 + lax.erf(pre_act * root_half))
    density = jnp.exp(-0.5 * pre_act * pre_act) * inv_root_tau
    return (
        pre_act * normal_cdf,
        normal_cdf + pre_act * density,
        density * (2.0 - pre_act * pre_act),
    )


def refresh(moment, curve, grad, hvp, tangent):
    moment_f = beta_first * moment.astype(F32) + (1.0 - beta_first) * grad
    curve_f = beta_second * curve.astype(F32) + (1.0 - beta_second) * tangent.astype(F32) * hvp
    step = jnp.clip(moment_f / jnp.maximum(gamma_scale * curve_f, ratio_floor), -1.0, 1.0)
    return step, moment_f.astype(BF16), curve_f.astype(BF16)


def wrap(value, size):
    return lax.rem(value + size, size)


class Here:
    def __init__(self):
        dp = lax.axis_index("dp")
        tensor = lax.axis_index("tensor")
        self.core = lax.rem(tensor, 2)
        self.pos = {
            "x": lax.rem(lax.div(dp, 8), 4),
            "z": lax.rem(dp, 8),
            "y": lax.div(tensor, 2) * 2 + lax.div(dp, 32),
        }
        self.me = self.core * 4 + self.pos["y"]
        self.steps = {
            (axis, by): wrap(self.pos[axis] + by, SIZE[axis])
            for axis in AXES
            for by in range(SIZE[axis])
        }
        self.devices = {
            key: self.device({**self.pos, key[0]: spot}, self.core)
            for key, spot in self.steps.items()
            if key[1]
        }
        self.sibling = self.device(self.pos, 1 - self.core)

    def device(self, pos, core):
        y = pos["y"]
        return (
            lax.rem(y, 2) * 32 + pos["x"] * 8 + pos["z"],
            lax.div(y, 2) * 2 + core,
        )

    def member(self, by):
        spot = lax.rem(self.me + by, GROUP)
        return self.device({**self.pos, "y": lax.rem(spot, 4)}, lax.div(spot, 4))

    def step(self, axis, by):
        return self.steps[(axis, by % SIZE[axis])]

    def beside(self, axis, by):
        return self.devices[(axis, by)]


def place(where):
    return tuple(where[axis] for axis in AXES)


def gather(buffer, here, sets, send_sems, recv_sems, sent, keep=None):
    side = keep is not None
    columns = pl.ds(0, MAIN if side else WIDE)
    mine = buffer.at[here.core]
    other = buffer.at[1 - here.core]

    def copy(index, source, into, target):
        return pltpu.make_async_remote_copy(
            src_ref=source,
            dst_ref=into,
            send_sem=send_sems.at[index],
            recv_sem=recv_sems.at[index],
            device_id=target,
            device_id_type=MESH,
        )

    def start(index, source, into, target):
        made = copy(index, source, into, target)
        made.start()
        sent.append(made)

    def set_block(q, m, f):
        part, row, rows = sets[q]
        middle, final = PARTS[part]
        where = {
            middle: here.step(middle, -m),
            final: here.step(final, -f),
            "z": pl.ds(row, rows),
        }
        return mine.at[place(where) + (slice(None), columns)]

    def launch(q):
        middle, final = PARTS[sets[q][0]]
        own = set_block(q, 0, 0)
        for m in NEAR:
            start(7 + q * 15 + m - 1, own, own, here.beside(middle, m))
        for f in NEAR:
            start(10 + q * 15 + f - 1, own, own, here.beside(final, f))

    def arrive(*offsets):
        for offset in offsets:
            where = place({**here.pos, "z": OFFSETS.index(offset)})
            came = mine.at[where + (slice(None), columns)]
            copy(7 - offset, came, came, here.sibling).wait_recv()

    def forward(q):
        final = PARTS[sets[q][0]][1]
        for m in (1, 3, 2):
            came = set_block(q, m, 0)
            copy(7 + q * 15 + m - 1, came, came, here.sibling).wait_recv()
            for f in NEAR:
                start(13 + q * 15 + (m - 1) * 3 + f - 1, came, came, here.beside(final, f))

    def finish(q):
        for m in (0, 1, 3, 2):
            for f in (1, 3, 2):
                index = (10 if m == 0 else 13 + (m - 1) * 3) + q * 15 + f - 1
                came = set_block(q, m, f)
                copy(index, came, came, here.sibling).wait_recv()

    def hand_on(number):
        row = PAIRS[number][1]
        ref = mine.at[:, :, row : row + 2, :, columns]
        start(97 + number, ref, ref, here.sibling)

    here_y, here_x = here.pos["y"], here.pos["x"]

    def side_x():
        ref = mine.at[here_y, here_x, 0, :, SIDE]
        for by in NEAR:
            start(102 + by - 1, ref, ref, here.beside("x", by))

    def side_y():
        for by in NEAR:
            ref = mine.at[here_y, here.step("x", -by), 0, :, SIDE]
            copy(102 + by - 1, ref, ref, here.sibling).wait_recv()
        ref = mine.at[here_y, :, 0, :, SIDE]
        for by in NEAR:
            start(105 + by - 1, ref, ref, here.beside("y", by))

    def side_z():
        for by in NEAR:
            ref = mine.at[here.step("y", -by), :, 0, :, SIDE]
            copy(105 + by - 1, ref, ref, here.sibling).wait_recv()
        for by in (4, 3, 5, 2, 6, 1, 7):
            into = mine.at[:, :, OFFSETS.index(8 - by), :, SIDE]
            start(108 + by - 1, mine.at[:, :, 0, :, SIDE], into, here.beside("z", by))

    def side_end():
        for by in (1, 7, 2, 6, 3, 5, 4):
            ref = mine.at[:, :, OFFSETS.index(8 - by), :, SIDE]
            copy(108 + by - 1, ref, ref, here.sibling).wait_recv()
        ref = mine.at[:, :, :, :, SIDE]
        start(101, ref, ref, here.sibling)
        keep(None, here.core)

    if side:
        side_x()
    own = mine.at[place({**here.pos, "z": 0}) + (slice(None), columns)]
    for by in (1, 7, 2, 6, 3, 5, 4):
        into = mine.at[place({**here.pos, "z": OFFSETS.index(8 - by)}) + (slice(None), columns)]
        start(by - 1, own, into, here.beside("z", by))
    if len(sets) == 6:
        launch(0)
        yield
        arrive(1)
        launch(1)
        side_y()
        arrive(7)
        launch(2)
        arrive(6)
        launch(3)
        forward(0)
        side_z()
        arrive(2, 3)
        launch(4)
        arrive(5, 4)
        launch(5)
        for q in (1, 2, 3, 4, 5):
            forward(q)
        completing = (1, 3, 4, 5)
    else:
        yield
        arrive(1)
        launch(0)
        arrive(7, 6)
        launch(1)
        arrive(2, 3)
        launch(2)
        arrive(5, 4)
        launch(3)
        for q in range(4):
            forward(q)
        completing = (0, 1, 2, 3)
    for q in range(len(sets)):
        finish(q)
        if side and q == 3:
            side_end()
        if q in completing:
            hand_on(completing.index(q))
            if keep is not None:
                keep(completing.index(q), here.core)
    for number, (_, row, rows) in enumerate(PAIRS):
        came = other.at[:, :, row : row + rows, :, columns]
        copy(97 + number, came, came, here.sibling).wait_recv()
        if keep is not None:
            keep(number, 1 - here.core)
    if side:
        came = other.at[:, :, :, :, SIDE]
        copy(101, came, came, here.sibling).wait_recv()
        keep(None, 1 - here.core)


class Scatter:
    def __init__(self, sums, boxes, here, send_sems, recv_sems, sent):
        self.sums, self.boxes, self.here = sums, boxes, here
        self.send_sems, self.recv_sems, self.sent = send_sems, recv_sems, sent

    def copy(self, index, source, into, target):
        return pltpu.make_async_remote_copy(
            src_ref=source,
            dst_ref=into,
            send_sem=self.send_sems.at[index],
            recv_sem=self.recv_sems.at[index],
            device_id=target,
            device_id_type=MESH,
        )

    def start(self, *what):
        made = self.copy(*what)
        made.start()
        self.sent.append(made)

    def rows(self, q):
        return pl.ds(PAIRS[q][1], PAIRS[q][2])

    def piece(self, q, by_first, by_second):
        second, first = PARTS[PAIRS[q][0]]
        where = {
            first: self.here.step(first, by_first),
            second: self.here.step(second, by_second),
            "z": self.rows(q),
        }
        return place(where) + (slice(None), pl.ds(0, MAIN))

    def first_x(self, q, by, by_second):
        self.start(
            q * 15 + (by - 1) * 4 + by_second,
            self.sums.at[self.piece(q, by, by_second)],
            self.boxes[0].at[by - 1, by_second, self.rows(q)],
            self.here.beside("x", by),
        )

    def first_y(self, q, by):
        self.start(
            q * 15 + by - 1,
            self.sums.at[self.here.step("y", by), :, self.rows(q), :, pl.ds(0, MAIN)],
            self.boxes[0].at[by - 1, :, self.rows(q)],
            self.here.beside("y", by),
        )

    def came(self, index, into):
        self.copy(index, into, into, self.here.sibling).wait_recv()

    def second(self, q, by_second, fresh):
        where = self.piece(q, 0, by_second)
        total = self.sums[where].astype(F32)
        rows = self.rows(q)
        for by in (1, 3, 2):
            if PAIRS[q][0] == 0:
                into = (by - 1, by_second, rows)
                self.came(q * 15 + (by - 1) * 4 + by_second, self.boxes[0].at[into])
            else:
                into = (by - 1, self.here.step("x", by_second), rows)
                if fresh:
                    self.came(q * 15 + by - 1, self.boxes[0].at[by - 1, :, rows])
            total = total + self.boxes[0][into].astype(F32)
        if by_second:
            self.sums[where] = total.astype(BF16)
            self.start(
                q * 15 + 12 + by_second - 1,
                self.sums.at[where],
                self.boxes[1].at[by_second - 1, rows],
                self.here.beside(PARTS[PAIRS[q][0]][0], by_second),
            )
            return
        for by in (1, 3, 2):
            into = (by - 1, rows)
            self.came(q * 15 + 12 + by - 1, self.boxes[1].at[into])
            total = total + self.boxes[1][into].astype(F32)
        self.sums[where] = total.astype(BF16)

    def third(self, *offsets):
        for by in offsets:
            self.start(
                60 + by - 1,
                self.sums.at[self.own(OFFSETS.index(by))],
                self.boxes[2].at[by - 1],
                self.here.beside("z", by),
            )

    def own(self, row):
        return place({**self.here.pos, "z": row}) + (slice(None), pl.ds(0, MAIN))

    def side_z(self, *offsets):
        for by in offsets:
            self.start(
                67 + by - 1,
                self.sums.at[:, :, OFFSETS.index(by), :, SIDE],
                self.boxes[3].at[by - 1],
                self.here.beside("z", by),
            )

    def side_y(self):
        total = self.sums[:, :, 0, :, SIDE].astype(F32)
        for by in (1, 7, 2, 6, 3, 5, 4):
            self.came(67 + by - 1, self.boxes[3].at[by - 1])
            total = total + self.boxes[3][by - 1].astype(F32)
        self.sums[:, :, 0, :, SIDE] = total.astype(BF16)
        for by in NEAR:
            self.start(
                74 + by - 1,
                self.sums.at[self.here.step("y", by), :, 0, :, SIDE],
                self.boxes[4].at[by - 1],
                self.here.beside("y", by),
            )

    def side_x(self):
        y = self.here.pos["y"]
        total = self.sums[y, :, 0, :, SIDE].astype(F32)
        for by in (1, 3, 2):
            self.came(74 + by - 1, self.boxes[4].at[by - 1])
            total = total + self.boxes[4][by - 1].astype(F32)
        self.sums[y, :, 0, :, SIDE] = total.astype(BF16)
        for by in NEAR:
            self.start(
                77 + by - 1,
                self.sums.at[y, self.here.step("x", by), 0, :, SIDE],
                self.boxes[5].at[by - 1],
                self.here.beside("x", by),
            )

    def side_total(self):
        total = self.sums[self.here.pos["y"], self.here.pos["x"], 0, :, SIDE].astype(F32)
        for by in (1, 3, 2):
            self.came(77 + by - 1, self.boxes[5].at[by - 1])
            total = total + self.boxes[5][by - 1].astype(F32)
        return total

    def total(self):
        total = self.sums[self.own(0)].astype(F32)
        for by in (4, 3, 5, 2, 6, 1, 7):
            self.came(60 + by - 1, self.boxes[2].at[by - 1])
            total = total + self.boxes[2][by - 1].astype(F32)
        return total


def kernel(
    tokens,
    target,
    master_up,
    master_down,
    tangent_up,
    tangent_down,
    tokens_out,
    residuals_out,
    both_t,
    grads_t,
    v_tokens,
    v_target,
    v_master_up,
    v_master_down,
    v_tangent_up,
    v_tangent_down,
    group,
    folded,
    all_tokens,
    weights_up,
    weights_down,
    acc,
    both,
    slopes_ref,
    bend_ref,
    outgoing,
    incoming,
    sums,
    residuals,
    *rest,
):
    boxes = rest[:6]
    in_sems, out_sems, pair_send, pair_recv, group_send, group_recv = rest[6:12]
    first_send, first_recv, scatter_send, scatter_recv, second_send, second_recv = rest[12:]

    here = Here()
    core, pos, me = here.core, here.pos, here.me
    sent = []

    barrier = pltpu.get_barrier_semaphore()
    peers = [here.member(by) for by in range(1, GROUP)]
    peers += [here.beside("x", by) for by in range(1, 4)]
    peers += [here.beside("z", by) for by in range(1, 8)]
    for peer in peers:
        pl.semaphore_signal(barrier, inc=1, device_id=peer, device_id_type=MESH)

    loads = []
    pairs = (
        (tokens, v_tokens),
        (target, v_target),
        (master_up, v_master_up),
        (tangent_up, v_tangent_up),
        (master_down, v_master_down),
        (tangent_down, v_tangent_down),
    )
    for number, (source, into) in enumerate(pairs):
        made = pltpu.make_async_copy(source, into, in_sems.at[number])
        made.start()
        loads.append(made)

    def fold(rows):
        rows = rows.astype(F32)
        pieces = [rows[:, k * WIDE : (k + 1) * WIDE] for k in range(GROUP)]
        return jnp.concatenate(pieces, axis=0).astype(BF16)

    loads[0].wait()
    loads[1].wait()
    folded[core, pos["y"], pos["x"], 0] = fold(v_tokens[...])
    group[me] = fold(v_target[...])

    loads[2].wait()
    loads[3].wait()
    zeros_up = jnp.zeros((PAD - HID, 768), BF16)
    for k in range(4):
        columns = slice(k * 768, (k + 1) * 768)
        weights_up[k, 0:HID] = v_master_up[:, columns].astype(BF16)
        weights_up[k, HID:PAD] = zeros_up
        weights_up[k, PAD : PAD + HID] = v_tangent_up[:, columns]
        weights_up[k, PAD + HID :] = zeros_up
    pl.semaphore_wait(barrier, len(peers))

    first = gather(folded, here, PAIRS, first_send, first_recv, sent)
    next(first)

    def group_copy(by, spot):
        return pltpu.make_async_remote_copy(
            src_ref=group.at[spot],
            dst_ref=group.at[spot],
            send_sem=group_send.at[by],
            recv_sem=group_recv.at[by],
            device_id=here.member(by),
            device_id_type=MESH,
        )

    for by in range(1, GROUP):
        made = group_copy(by, me)
        made.start()
        sent.append(made)

    loads[4].wait()
    loads[5].wait()
    zeros_low = jnp.zeros((PAD - HID, 2 * WIDE), BF16)
    zeros_half = jnp.zeros((HID, WIDE), BF16)
    for spot in range(GROUP):
        columns = slice(spot * WIDE, (spot + 1) * WIDE)
        weight = v_master_down[:, columns].astype(BF16)
        weights_down[spot, 0:HID, 0:WIDE] = weight
        weights_down[spot, 0:HID, WIDE:] = v_tangent_down[:, columns]
        weights_down[spot, HID:PAD] = zeros_low
        weights_down[spot, PAD : PAD + HID, 0:WIDE] = zeros_half
        weights_down[spot, PAD : PAD + HID, WIDE:] = weight
        weights_down[spot, PAD + HID :] = zeros_low

    for _ in first:
        pass

    row = lax.broadcasted_iota(jnp.int32, (128, 128), 0)
    column = lax.broadcasted_iota(jnp.int32, (128, 128), 1)
    token = lax.rem(row, 16)
    pick = column == lax.div(token, 2) * 16 + lax.div(row, 16) * 2 + lax.rem(token, 2)
    pick = pick.astype(F32).astype(BF16)

    @pl.loop(0, 4)
    def _(x):
        for z in range(8):
            blocks = folded[:, :, x, z].reshape(128, WIDE)
            rows = jnp.dot(pick, blocks, preferred_element_type=F32).astype(BF16)
            all_tokens[:, x, z] = rows.reshape(GROUP, 16, WIDE)

    stores = [pltpu.make_async_copy(all_tokens, tokens_out, out_sems.at[0])]
    stores[0].start()

    acc[...] = jnp.zeros_like(acc)

    @pl.loop(0, 4)
    def _(k):
        blocks = [all_tokens[2 * k + lower].reshape(TOKENS, WIDE) for lower in range(2)]
        acc[...] += lax.dot_general(
            jnp.concatenate(blocks, axis=1),
            weights_up[k],
            (((1,), (1,)), ((), ())),
            preferred_element_type=F32,
        )

    @pl.loop(0, 4)
    def _(x):
        span = pl.ds(pl.multiple_of(x * 128, 128), 128)
        pre_tangent = acc[span, PAD:]
        activated, slopes, bending = gelu_parts(acc[span, :PAD])
        slopes_ref[span] = slopes
        bend_ref[span] = bending * pre_tangent
        pair = jnp.concatenate([activated, slopes * pre_tangent], axis=1)
        both[x] = pair.astype(BF16).reshape(8, 16, 2 * PAD)

    def pair_copy(far, by):
        return pltpu.make_async_remote_copy(
            src_ref=outgoing.at[far, by],
            dst_ref=incoming.at[far, by],
            send_sem=pair_send.at[far, by],
            recv_sem=pair_recv.at[far, by],
            device_id=here.sibling,
            device_id_type=MESH,
        )

    turns = (1, 3, 2, 0)
    shape = (4, 4, 16, 2 * WIDE)

    def product(far, spot):
        left = both[:, 4 * far : 4 * far + 4].reshape(TOKENS // 2, 2 * PAD)
        return jnp.dot(left, weights_down[spot], preferred_element_type=F32)

    scatter = Scatter(sums, boxes, here, scatter_send, scatter_recv, sent)
    for far in (1, 0):
        for by in turns:
            spot = (1 - core) * 4 + here.step("y", by)
            outgoing[far, by] = product(far, spot).astype(BF16).reshape(shape)
            made = pair_copy(far, by)
            made.start()
            sent.append(made)
        for by in turns:
            pair_copy(far, by).wait_recv()
            y = here.step("y", by)
            block = product(far, core * 4 + y)
            block = block + incoming[far, by].astype(F32).reshape(TOKENS // 2, 2 * WIDE)
            sums[y, :, 4 * far : 4 * far + 4] = block.astype(BF16).reshape(shape)
            for to in NEAR:
                scatter.first_x(2 * far, to, by)
            if by:
                scatter.first_y(2 * far + 1, by)
        scatter.side_z(*((4, 3, 5, 2) if far else (6, 1, 7)))

    both_t[...] = both[...].reshape(TOKENS, 2 * PAD).astype(F32).T.astype(BF16)
    for by in turns:
        for q in (2, 3):
            scatter.second(q, by, by == turns[0])
    scatter.third(4, 3, 5, 2)
    for by in turns:
        for q in (1, 0):
            scatter.second(q, by, by == turns[0])
            if by == 0:
                scatter.third(*((6, 7) if q else (1,)))
        if by == 3:
            scatter.side_y()
    scatter.side_x()
    total = scatter.total()
    total = jnp.concatenate([total, scatter.side_total()], axis=1)

    for by in range(1, GROUP):
        group_copy(by, lax.rem(me + GROUP - by, GROUP)).wait_recv()
    row = lax.broadcasted_iota(jnp.int32, (16, 128), 0)
    column = lax.broadcasted_iota(jnp.int32, (16, 128), 1)
    pick = (column == lax.div(row, 2) * 16 + me * 2 + lax.rem(row, 2)).astype(F32).astype(BF16)
    goal = jnp.dot(pick, group[...].reshape(128, WIDE), preferred_element_type=F32)
    pair = jnp.concatenate([total[:, WIDE:], total[:, :WIDE] - goal], axis=1)
    residuals[core, pos["y"], pos["x"], 0] = pair.astype(BF16)

    def keep(number, core):
        row, rows, columns = 0, 8, SIDE
        if number is not None:
            row, rows, columns = PAIRS[number][1], 2, pl.ds(0, MAIN)
        made = pltpu.make_async_copy(
            residuals.at[core, :, :, row : row + rows, :, columns],
            residuals_out.at[core, :, :, row : row + rows, :, columns],
            out_sems.at[len(stores)],
        )
        made.start()
        stores.append(made)

    earlier = list(sent)
    sent.clear()
    last = gather(residuals, here, SETS, second_send, second_recv, sent, keep)
    next(last)
    for made in earlier:
        made.wait_send()
    for _ in last:
        pass

    acc[...] = jnp.zeros_like(acc)

    @pl.loop(0, GROUP)
    def _(spot):
        acc[...] += lax.dot_general(
            residuals[lax.div(spot, 4), lax.rem(spot, 4)].reshape(TOKENS, 2 * WIDE),
            weights_down[spot],
            (((1,), (1,)), ((), ())),
            preferred_element_type=F32,
        )

    for k in range(4):
        span = slice(k * 128, (k + 1) * 128)
        back_dot, back_grad = acc[span, :PAD], acc[span, PAD:]
        slopes = slopes_ref[span]
        grad_pre = (back_grad * slopes).T.astype(BF16)
        grad_pre_dot = (back_dot * slopes + back_grad * bend_ref[span]).T.astype(BF16)
        grads_t[0:PAD, span] = grad_pre
        grads_t[PAD:, span] = grad_pre_dot

    for made in stores:
        made.wait()
    for made in sent:
        made.wait_send()


def update(
    grads_t,
    both_t,
    tokens,
    residuals,
    tangent_up,
    tangent_down,
    moment_up,
    moment_down,
    curve_up,
    curve_down,
    step_up,
    step_down,
    moment_up_next,
    moment_down_next,
    curve_up_next,
    curve_down_next,
):
    first = 2 * pl.program_id(0)
    loss_scale = 1.0 / math.sqrt(TOKENS)
    wide = [tokens[first + k].reshape(TOKENS, WIDE) for k in range(2)]
    up = jnp.dot(grads_t[...], jnp.concatenate(wide, axis=1), preferred_element_type=F32)
    step_up[...], moment_up_next[...], curve_up_next[...] = refresh(
        moment_up[...],
        curve_up[...],
        loss_scale * up[:HID],
        loss_scale * up[PAD : PAD + HID],
        tangent_up[...],
    )
    grad, hvp = [], []
    for k in range(2):
        down = jnp.dot(
            both_t[...],
            residuals[first + k].reshape(TOKENS, 2 * WIDE),
            preferred_element_type=F32,
        )
        grad.append(down[:HID, WIDE:])
        hvp.append(down[:HID, :WIDE] + down[PAD : PAD + HID, WIDE:])
    step_down[...], moment_down_next[...], curve_down_next[...] = refresh(
        moment_down[...],
        curve_down[...],
        loss_scale * jnp.concatenate(grad, axis=1),
        loss_scale * jnp.concatenate(hvp, axis=1),
        tangent_down[...],
    )


def per_device(
    tokens,
    target,
    master_up,
    master_down,
    tangent_up,
    tangent_down,
    moment_up,
    moment_down,
    curve_up,
    curve_down,
):
    wide32 = jax.ShapeDtypeStruct((HID, D), F32)
    wide16 = jax.ShapeDtypeStruct((HID, D), BF16)
    blocks = (4, 4, 8, 16)
    any_spec = pl.BlockSpec(memory_space=pl.ANY)
    vmem_spec = pl.BlockSpec(memory_space=pltpu.VMEM)
    scratch = [pltpu.VMEM((2, D), BF16)] * 2
    scratch += [pltpu.VMEM((HID, D), F32)] * 2 + [pltpu.VMEM((HID, D), BF16)] * 2
    scratch += [
        pltpu.VMEM((GROUP, 16, WIDE), BF16),
        pltpu.VMEM((2,) + blocks + (WIDE,), BF16),
        pltpu.VMEM((GROUP, 4, 8, 16, WIDE), BF16),
        pltpu.VMEM((4, 2 * PAD, 768), BF16),
        pltpu.VMEM((GROUP, 2 * PAD, 2 * WIDE), BF16),
        pltpu.VMEM((TOKENS, 2 * PAD), F32),
        pltpu.VMEM((4, 8, 16, 2 * PAD), BF16),
        pltpu.VMEM((TOKENS, PAD), F32),
        pltpu.VMEM((TOKENS, PAD), F32),
        pltpu.VMEM((2, 4, 4, 4, 16, 2 * WIDE), BF16),
        pltpu.VMEM((2, 4, 4, 4, 16, 2 * WIDE), BF16),
        pltpu.VMEM(blocks + (2 * WIDE,), BF16),
        pltpu.VMEM((2,) + blocks + (2 * WIDE,), BF16),
        pltpu.VMEM((3, 4, 8, 16, MAIN), BF16),
        pltpu.VMEM((3, 8, 16, MAIN), BF16),
        pltpu.VMEM((7, 16, MAIN), BF16),
        pltpu.VMEM((7, 4, 4, 16, 2 * WIDE - MAIN), BF16),
        pltpu.VMEM((3, 4, 16, 2 * WIDE - MAIN), BF16),
        pltpu.VMEM((3, 16, 2 * WIDE - MAIN), BF16),
    ]
    dma = pltpu.SemaphoreType.DMA
    scratch += [
        dma((6,)),
        dma((11,)),
        dma((2, 4)),
        dma((2, 4)),
        dma((GROUP,)),
        dma((GROUP,)),
        dma((GATHER_COUNT,)),
        dma((GATHER_COUNT,)),
        dma((SCATTER_COUNT,)),
        dma((SCATTER_COUNT,)),
        dma((GATHER_COUNT,)),
        dma((GATHER_COUNT,)),
    ]
    all_tokens, residuals, both_t, grads_t = pl.pallas_call(
        kernel,
        out_shape=(
            pltpu.VMEM((GROUP, 4, 8, 16, WIDE), BF16),
            pltpu.VMEM((2,) + blocks + (2 * WIDE,), BF16),
            pltpu.VMEM((2 * PAD, TOKENS), BF16),
            pltpu.VMEM((2 * PAD, TOKENS), BF16),
        ),
        in_specs=[any_spec] * 6,
        out_specs=(vmem_spec,) * 4,
        scratch_shapes=scratch,
        compiler_params=pltpu.CompilerParams(
            collective_id=0, has_side_effects=True, vmem_limit_bytes=49 * 1024 * 1024
        ),
        cost_estimate=pl.CostEstimate(
            flops=3_000_000_000, bytes_accessed=16_000_000, transcendentals=131072
        ),
    )(tokens, target, master_up, master_down, tangent_up, tangent_down)
    residuals = residuals.reshape((GROUP, 4, 8, 16, 2 * WIDE))
    whole = pl.BlockSpec((2 * PAD, TOKENS), lambda spot: (0, 0))
    part = pl.BlockSpec((HID, 2 * WIDE), lambda spot: (0, spot))
    return pl.pallas_call(
        update,
        grid=(GROUP // 2,),
        out_shape=(wide32, wide32, wide16, wide16, wide16, wide16),
        in_specs=[
            whole,
            whole,
            vmem_spec,
            vmem_spec,
        ]
        + [part] * 6,
        out_specs=(part,) * 6,
        compiler_params=pltpu.CompilerParams(vmem_limit_bytes=30 * 1024 * 1024),
        cost_estimate=pl.CostEstimate(
            flops=1_500_000_000, bytes_accessed=18_000_000, transcendentals=0
        ),
    )(
        grads_t,
        both_t,
        all_tokens,
        residuals,
        tangent_up,
        tangent_down,
        moment_up,
        moment_down,
        curve_up,
        curve_down,
    )


def solution(mesh):
    rows = P(("dp", "tensor"), None)
    return jax.shard_map(
        per_device, mesh=mesh, in_specs=(rows,) * 10, out_specs=(rows,) * 6, check_vma=False
    )
```

```python
import math

import jax
import jax.numpy as jnp
from jax import lax
from jax.experimental import pallas as pl
from jax.experimental.pallas import tpu as pltpu
from jax.sharding import PartitionSpec as P

TOKENS = 512
D = 3072
HID = 96
PAD = 128
PARTS = 3
SIZE = {"y": 4, "x": 4, "z": 8}
AXES = ("y", "x", "z")
GROUP = 8
WIDE = D // GROUP
NEAR = (2, 1, 3)
PARTS = (("y", "x"), ("x", "y"))
OFFSETS = (0, 1, 7, 6, 2, 3, 5, 4)
PAIRS = ((0, 0, 2), (1, 2, 2), (0, 4, 2), (1, 6, 2))
SETS = ((0, 0, 1), (0, 1, 1), (1, 2, 1), (1, 3, 1), (0, 4, 2), (1, 6, 2))
MAIN = 640
SIDE = pl.ds(MAIN, 2 * WIDE - MAIN)
GATHER_COUNT = 7 + 6 * 15 + 4 + 1 + 3 + 3 + 7
SCATTER_COUNT = 4 * 15 + 7 + 7 + 3 + 3

beta_first = 0.965
beta_second = 0.99
gamma_scale = 0.01
ratio_floor = 0.01
root_half = 0.7071067811865476
inv_root_tau = 0.3989422804014327

F32 = jnp.float32
BF16 = jnp.bfloat16
MESH = pl.DeviceIdType.MESH


def gelu_parts(pre_act):
    normal_cdf = 0.5 * (1.0 + lax.erf(pre_act * root_half))
    density = jnp.exp(-0.5 * pre_act * pre_act) * inv_root_tau
    return (
        pre_act * normal_cdf,
        normal_cdf + pre_act * density,
        density * (2.0 - pre_act * pre_act),
    )


def refresh(moment, curve, grad, hvp, tangent):
    moment_f = beta_first * moment.astype(F32) + (1.0 - beta_first) * grad
    curve_f = beta_second * curve.astype(F32) + (1.0 - beta_second) * tangent.astype(F32) * hvp
    step = jnp.clip(moment_f / jnp.maximum(gamma_scale * curve_f, ratio_floor), -1.0, 1.0)
    return step, moment_f.astype(BF16), curve_f.astype(BF16)


def wrap(value, size):
    return lax.rem(value + size, size)


class Here:
    def __init__(self):
        dp = lax.axis_index("dp")
        tensor = lax.axis_index("tensor")
        self.core = lax.rem(tensor, 2)
        self.pos = {
            "x": lax.rem(lax.div(dp, 8), 4),
            "z": lax.rem(dp, 8),
            "y": lax.div(tensor, 2) * 2 + lax.div(dp, 32),
        }
        self.me = self.core * 4 + self.pos["y"]
        self.steps = {
            (axis, by): wrap(self.pos[axis] + by, SIZE[axis])
            for axis in AXES
            for by in range(SIZE[axis])
        }
        self.devices = {
            key: self.device({**self.pos, key[0]: spot}, self.core)
            for key, spot in self.steps.items()
            if key[1]
        }
        self.sibling = self.device(self.pos, 1 - self.core)

    def device(self, pos, core):
        y = pos["y"]
        return (
            lax.rem(y, 2) * 32 + pos["x"] * 8 + pos["z"],
            lax.div(y, 2) * 2 + core,
        )

    def member(self, by):
        spot = lax.rem(self.me + by, GROUP)
        return self.device({**self.pos, "y": lax.rem(spot, 4)}, lax.div(spot, 4))

    def step(self, axis, by):
        return self.steps[(axis, by % SIZE[axis])]

    def beside(self, axis, by):
        return self.devices[(axis, by)]


def place(where):
    return tuple(where[axis] for axis in AXES)


def gather(buffer, here, sets, send_sems, recv_sems, sent, keep=None):
    side = keep is not None
    columns = pl.ds(0, MAIN if side else WIDE)
    mine = buffer.at[here.core]
    other = buffer.at[1 - here.core]

    def copy(index, source, into, target):
        return pltpu.make_async_remote_copy(
            src_ref=source,
            dst_ref=into,
            send_sem=send_sems.at[index],
            recv_sem=recv_sems.at[index],
            device_id=target,
            device_id_type=MESH,
        )

    def start(index, source, into, target):
        made = copy(index, source, into, target)
        made.start()
        sent.append(made)

    def set_block(q, m, f):
        part, row, rows = sets[q]
        middle, final = PARTS[part]
        where = {
            middle: here.step(middle, -m),
            final: here.step(final, -f),
            "z": pl.ds(row, rows),
        }
        return mine.at[place(where) + (slice(None), columns)]

    def launch(q):
        middle, final = PARTS[sets[q][0]]
        own = set_block(q, 0, 0)
        for m in NEAR:
            start(7 + q * 15 + m - 1, own, own, here.beside(middle, m))
        for f in NEAR:
            start(10 + q * 15 + f - 1, own, own, here.beside(final, f))

    def arrive(*offsets):
        for offset in offsets:
            where = place({**here.pos, "z": OFFSETS.index(offset)})
            came = mine.at[where + (slice(None), columns)]
            copy(7 - offset, came, came, here.sibling).wait_recv()

    def forward(q):
        final = PARTS[sets[q][0]][1]
        for m in (1, 3, 2):
            came = set_block(q, m, 0)
            copy(7 + q * 15 + m - 1, came, came, here.sibling).wait_recv()
            for f in NEAR:
                start(13 + q * 15 + (m - 1) * 3 + f - 1, came, came, here.beside(final, f))

    def finish(q):
        for m in (0, 1, 3, 2):
            for f in (1, 3, 2):
                index = (10 if m == 0 else 13 + (m - 1) * 3) + q * 15 + f - 1
                came = set_block(q, m, f)
                copy(index, came, came, here.sibling).wait_recv()

    def hand_on(number):
        row = PAIRS[number][1]
        ref = mine.at[:, :, row : row + 2, :, columns]
        start(97 + number, ref, ref, here.sibling)

    here_y, here_x = here.pos["y"], here.pos["x"]

    def side_x():
        ref = mine.at[here_y, here_x, 0, :, SIDE]
        for by in NEAR:
            start(102 + by - 1, ref, ref, here.beside("x", by))

    def side_y():
        for by in NEAR:
            ref = mine.at[here_y, here.step("x", -by), 0, :, SIDE]
            copy(102 + by - 1, ref, ref, here.sibling).wait_recv()
        ref = mine.at[here_y, :, 0, :, SIDE]
        for by in NEAR:
            start(105 + by - 1, ref, ref, here.beside("y", by))

    def side_z():
        for by in NEAR:
            ref = mine.at[here.step("y", -by), :, 0, :, SIDE]
            copy(105 + by - 1, ref, ref, here.sibling).wait_recv()
        for by in (4, 3, 5, 2, 6, 1, 7):
            into = mine.at[:, :, OFFSETS.index(8 - by), :, SIDE]
            start(108 + by - 1, mine.at[:, :, 0, :, SIDE], into, here.beside("z", by))

    def side_end():
        for by in (1, 7, 2, 6, 3, 5, 4):
            ref = mine.at[:, :, OFFSETS.index(8 - by), :, SIDE]
            copy(108 + by - 1, ref, ref, here.sibling).wait_recv()
        ref = mine.at[:, :, :, :, SIDE]
        start(101, ref, ref, here.sibling)
        keep(None, here.core)

    if side:
        side_x()
    own = mine.at[place({**here.pos, "z": 0}) + (slice(None), columns)]
    for by in (1, 7, 2, 6, 3, 5, 4):
        into = mine.at[place({**here.pos, "z": OFFSETS.index(8 - by)}) + (slice(None), columns)]
        start(by - 1, own, into, here.beside("z", by))
    if len(sets) == 6:
        launch(0)
        yield
        arrive(1)
        launch(1)
        side_y()
        arrive(7)
        launch(2)
        arrive(6)
        launch(3)
        forward(0)
        side_z()
        arrive(2, 3)
        launch(4)
        arrive(5, 4)
        launch(5)
        for q in (1, 2, 3, 4, 5):
            forward(q)
        completing = (1, 3, 4, 5)
    else:
        yield
        arrive(1)
        launch(0)
        arrive(7, 6)
        launch(1)
        arrive(2, 3)
        launch(2)
        arrive(5, 4)
        launch(3)
        for q in range(4):
            forward(q)
        completing = (0, 1, 2, 3)
    for q in range(len(sets)):
        finish(q)
        if side and q == 3:
            side_end()
        if q in completing:
            hand_on(completing.index(q))
            if keep is not None:
                keep(completing.index(q), here.core)
    for number, (_, row, rows) in enumerate(PAIRS):
        came = other.at[:, :, row : row + rows, :, columns]
        copy(97 + number, came, came, here.sibling).wait_recv()
        if keep is not None:
            keep(number, 1 - here.core)
    if side:
        came = other.at[:, :, :, :, SIDE]
        copy(101, came, came, here.sibling).wait_recv()
        keep(None, 1 - here.core)


class Scatter:
    def __init__(self, sums, boxes, here, send_sems, recv_sems, sent):
        self.sums, self.boxes, self.here = sums, boxes, here
        self.send_sems, self.recv_sems, self.sent = send_sems, recv_sems, sent

    def copy(self, index, source, into, target):
        return pltpu.make_async_remote_copy(
            src_ref=source,
            dst_ref=into,
            send_sem=self.send_sems.at[index],
            recv_sem=self.recv_sems.at[index],
            device_id=target,
            device_id_type=MESH,
        )

    def start(self, *what):
        made = self.copy(*what)
        made.start()
        self.sent.append(made)

    def rows(self, q):
        return pl.ds(PAIRS[q][1], PAIRS[q][2])

    def piece(self, q, by_first, by_second):
        second, first = PARTS[PAIRS[q][0]]
        where = {
            first: self.here.step(first, by_first),
            second: self.here.step(second, by_second),
            "z": self.rows(q),
        }
        return place(where) + (slice(None), pl.ds(0, MAIN))

    def first_x(self, q, by, by_second):
        self.start(
            q * 15 + (by - 1) * 4 + by_second,
            self.sums.at[self.piece(q, by, by_second)],
            self.boxes[0].at[by - 1, by_second, self.rows(q)],
            self.here.beside("x", by),
        )

    def first_y(self, q, by):
        self.start(
            q * 15 + by - 1,
            self.sums.at[self.here.step("y", by), :, self.rows(q), :, pl.ds(0, MAIN)],
            self.boxes[0].at[by - 1, :, self.rows(q)],
            self.here.beside("y", by),
        )

    def came(self, index, into):
        self.copy(index, into, into, self.here.sibling).wait_recv()

    def second(self, q, by_second, fresh):
        where = self.piece(q, 0, by_second)
        total = self.sums[where].astype(F32)
        rows = self.rows(q)
        for by in (1, 3, 2):
            if PAIRS[q][0] == 0:
                into = (by - 1, by_second, rows)
                self.came(q * 15 + (by - 1) * 4 + by_second, self.boxes[0].at[into])
            else:
                into = (by - 1, self.here.step("x", by_second), rows)
                if fresh:
                    self.came(q * 15 + by - 1, self.boxes[0].at[by - 1, :, rows])
            total = total + self.boxes[0][into].astype(F32)
        if by_second:
            self.sums[where] = total.astype(BF16)
            self.start(
                q * 15 + 12 + by_second - 1,
                self.sums.at[where],
                self.boxes[1].at[by_second - 1, rows],
                self.here.beside(PARTS[PAIRS[q][0]][0], by_second),
            )
            return
        for by in (1, 3, 2):
            into = (by - 1, rows)
            self.came(q * 15 + 12 + by - 1, self.boxes[1].at[into])
            total = total + self.boxes[1][into].astype(F32)
        self.sums[where] = total.astype(BF16)

    def third(self, *offsets):
        for by in offsets:
            self.start(
                60 + by - 1,
                self.sums.at[self.own(OFFSETS.index(by))],
                self.boxes[2].at[by - 1],
                self.here.beside("z", by),
            )

    def own(self, row):
        return place({**self.here.pos, "z": row}) + (slice(None), pl.ds(0, MAIN))

    def side_z(self, *offsets):
        for by in offsets:
            self.start(
                67 + by - 1,
                self.sums.at[:, :, OFFSETS.index(by), :, SIDE],
                self.boxes[3].at[by - 1],
                self.here.beside("z", by),
            )

    def side_y(self):
        total = self.sums[:, :, 0, :, SIDE].astype(F32)
        for by in (1, 7, 2, 6, 3, 5, 4):
            self.came(67 + by - 1, self.boxes[3].at[by - 1])
            total = total + self.boxes[3][by - 1].astype(F32)
        self.sums[:, :, 0, :, SIDE] = total.astype(BF16)
        for by in NEAR:
            self.start(
                74 + by - 1,
                self.sums.at[self.here.step("y", by), :, 0, :, SIDE],
                self.boxes[4].at[by - 1],
                self.here.beside("y", by),
            )

    def side_x(self):
        y = self.here.pos["y"]
        total = self.sums[y, :, 0, :, SIDE].astype(F32)
        for by in (1, 3, 2):
            self.came(74 + by - 1, self.boxes[4].at[by - 1])
            total = total + self.boxes[4][by - 1].astype(F32)
        self.sums[y, :, 0, :, SIDE] = total.astype(BF16)
        for by in NEAR:
            self.start(
                77 + by - 1,
                self.sums.at[y, self.here.step("x", by), 0, :, SIDE],
                self.boxes[5].at[by - 1],
                self.here.beside("x", by),
            )

    def side_total(self):
        total = self.sums[self.here.pos["y"], self.here.pos["x"], 0, :, SIDE].astype(F32)
        for by in (1, 3, 2):
            self.came(77 + by - 1, self.boxes[5].at[by - 1])
            total = total + self.boxes[5][by - 1].astype(F32)
        return total

    def total(self):
        total = self.sums[self.own(0)].astype(F32)
        for by in (4, 3, 5, 2, 6, 1, 7):
            self.came(60 + by - 1, self.boxes[2].at[by - 1])
            total = total + self.boxes[2][by - 1].astype(F32)
        return total


def kernel(
    tokens,
    target,
    master_up,
    master_down,
    tangent_up,
    tangent_down,
    tokens_out,
    residuals_out,
    both_t,
    grads_t,
    v_tokens,
    v_target,
    v_master_up,
    v_master_down,
    v_tangent_up,
    v_tangent_down,
    group,
    folded,
    all_tokens,
    weights_up,
    weights_down,
    acc,
    both,
    slopes_ref,
    bend_ref,
    outgoing,
    incoming,
    sums,
    residuals,
    *rest,
):
    boxes = rest[:6]
    in_sems, out_sems, pair_send, pair_recv, group_send, group_recv = rest[6:12]
    first_send, first_recv, scatter_send, scatter_recv, second_send, second_recv = rest[12:]

    here = Here()
    core, pos, me = here.core, here.pos, here.me
    sent = []

    barrier = pltpu.get_barrier_semaphore()
    peers = [here.member(by) for by in range(1, GROUP)]
    peers += [here.beside("x", by) for by in range(1, 4)]
    peers += [here.beside("z", by) for by in range(1, 8)]
    for peer in peers:
        pl.semaphore_signal(barrier, inc=1, device_id=peer, device_id_type=MESH)

    loads = []
    pairs = (
        (tokens, v_tokens),
        (target, v_target),
        (master_up, v_master_up),
        (tangent_up, v_tangent_up),
        (master_down, v_master_down),
        (tangent_down, v_tangent_down),
    )
    for number, (source, into) in enumerate(pairs):
        made = pltpu.make_async_copy(source, into, in_sems.at[number])
        made.start()
        loads.append(made)

    def fold(rows):
        rows = rows.astype(F32)
        pieces = [rows[:, k * WIDE : (k + 1) * WIDE] for k in range(GROUP)]
        return jnp.concatenate(pieces, axis=0).astype(BF16)

    loads[0].wait()
    loads[1].wait()
    folded[core, pos["y"], pos["x"], 0] = fold(v_tokens[...])
    group[me] = fold(v_target[...])

    loads[2].wait()
    loads[3].wait()
    zeros_up = jnp.zeros((PAD - HID, 768), BF16)
    for k in range(4):
        columns = slice(k * 768, (k + 1) * 768)
        weights_up[k, 0:HID] = v_master_up[:, columns].astype(BF16)
        weights_up[k, HID:PAD] = zeros_up
        weights_up[k, PAD : PAD + HID] = v_tangent_up[:, columns]
        weights_up[k, PAD + HID :] = zeros_up
    pl.semaphore_wait(barrier, len(peers))

    first = gather(folded, here, PAIRS, first_send, first_recv, sent)
    next(first)

    def group_copy(by, spot):
        return pltpu.make_async_remote_copy(
            src_ref=group.at[spot],
            dst_ref=group.at[spot],
            send_sem=group_send.at[by],
            recv_sem=group_recv.at[by],
            device_id=here.member(by),
            device_id_type=MESH,
        )

    for by in range(1, GROUP):
        made = group_copy(by, me)
        made.start()
        sent.append(made)

    loads[4].wait()
    loads[5].wait()
    zeros_low = jnp.zeros((PAD - HID, 2 * WIDE), BF16)
    zeros_half = jnp.zeros((HID, WIDE), BF16)
    for spot in range(GROUP):
        columns = slice(spot * WIDE, (spot + 1) * WIDE)
        weight = v_master_down[:, columns].astype(BF16)
        weights_down[spot, 0:HID, 0:WIDE] = weight
        weights_down[spot, 0:HID, WIDE:] = v_tangent_down[:, columns]
        weights_down[spot, HID:PAD] = zeros_low
        weights_down[spot, PAD : PAD + HID, 0:WIDE] = zeros_half
        weights_down[spot, PAD : PAD + HID, WIDE:] = weight
        weights_down[spot, PAD + HID :] = zeros_low

    for _ in first:
        pass

    row = lax.broadcasted_iota(jnp.int32, (128, 128), 0)
    column = lax.broadcasted_iota(jnp.int32, (128, 128), 1)
    token = lax.rem(row, 16)
    pick = column == lax.div(token, 2) * 16 + lax.div(row, 16) * 2 + lax.rem(token, 2)
    pick = pick.astype(F32).astype(BF16)

    @pl.loop(0, 4)
    def _(x):
        for z in range(8):
            blocks = folded[:, :, x, z].reshape(128, WIDE)
            rows = jnp.dot(pick, blocks, preferred_element_type=F32).astype(BF16)
            all_tokens[:, x, z] = rows.reshape(GROUP, 16, WIDE)

    stores = [pltpu.make_async_copy(all_tokens, tokens_out, out_sems.at[0])]
    stores[0].start()

    acc[...] = jnp.zeros_like(acc)

    @pl.loop(0, 4)
    def _(k):
        blocks = [all_tokens[2 * k + lower].reshape(TOKENS, WIDE) for lower in range(2)]
        acc[...] += lax.dot_general(
            jnp.concatenate(blocks, axis=1),
            weights_up[k],
            (((1,), (1,)), ((), ())),
            preferred_element_type=F32,
        )

    @pl.loop(0, 4)
    def _(x):
        span = pl.ds(pl.multiple_of(x * 128, 128), 128)
        pre_tangent = acc[span, PAD:]
        activated, slopes, bending = gelu_parts(acc[span, :PAD])
        slopes_ref[span] = slopes
        bend_ref[span] = bending * pre_tangent
        pair = jnp.concatenate([activated, slopes * pre_tangent], axis=1)
        both[x] = pair.astype(BF16).reshape(8, 16, 2 * PAD)

    def pair_copy(far, by):
        return pltpu.make_async_remote_copy(
            src_ref=outgoing.at[far, by],
            dst_ref=incoming.at[far, by],
            send_sem=pair_send.at[far, by],
            recv_sem=pair_recv.at[far, by],
            device_id=here.sibling,
            device_id_type=MESH,
        )

    turns = (1, 3, 2, 0)
    shape = (4, 4, 16, 2 * WIDE)

    def product(far, spot):
        left = both[:, 4 * far : 4 * far + 4].reshape(TOKENS // 2, 2 * PAD)
        return jnp.dot(left, weights_down[spot], preferred_element_type=F32)

    scatter = Scatter(sums, boxes, here, scatter_send, scatter_recv, sent)
    for far in (1, 0):
        for by in turns:
            spot = (1 - core) * 4 + here.step("y", by)
            outgoing[far, by] = product(far, spot).astype(BF16).reshape(shape)
            made = pair_copy(far, by)
            made.start()
            sent.append(made)
        for by in turns:
            pair_copy(far, by).wait_recv()
            y = here.step("y", by)
            block = product(far, core * 4 + y)
            block = block + incoming[far, by].astype(F32).reshape(TOKENS // 2, 2 * WIDE)
            sums[y, :, 4 * far : 4 * far + 4] = block.astype(BF16).reshape(shape)
            for to in NEAR:
                scatter.first_x(2 * far, to, by)
            if by:
                scatter.first_y(2 * far + 1, by)
        scatter.side_z(*((4, 3, 5, 2) if far else (6, 1, 7)))

    for by in range(1, GROUP):
        group_copy(by, lax.rem(me + GROUP - by, GROUP)).wait_recv()
    row = lax.broadcasted_iota(jnp.int32, (16, 128), 0)
    column = lax.broadcasted_iota(jnp.int32, (16, 128), 1)
    pick = (column == lax.div(row, 2) * 16 + me * 2 + lax.rem(row, 2)).astype(F32).astype(BF16)
    goal = jnp.dot(pick, group[...].reshape(128, WIDE), preferred_element_type=F32)
    both_t[...] = both[...].reshape(TOKENS, 2 * PAD).astype(F32).T.astype(BF16)
    for by in turns:
        for q in (2, 3):
            scatter.second(q, by, by == turns[0])
    scatter.third(4, 3, 5, 2)
    for by in turns:
        for q in (1, 0):
            scatter.second(q, by, by == turns[0])
            if by == 0:
                scatter.third(*((6, 7) if q else (1,)))
        if by == 3:
            scatter.side_y()
    scatter.side_x()
    total = scatter.total()
    total = jnp.concatenate([total, scatter.side_total()], axis=1)

    pair = jnp.concatenate([total[:, WIDE:], total[:, :WIDE] - goal], axis=1)
    residuals[core, pos["y"], pos["x"], 0] = pair.astype(BF16)

    def keep(number, core):
        row, rows, columns = 0, 8, SIDE
        if number is not None:
            row, rows, columns = PAIRS[number][1], 2, pl.ds(0, MAIN)
        made = pltpu.make_async_copy(
            residuals.at[core, :, :, row : row + rows, :, columns],
            residuals_out.at[core, :, :, row : row + rows, :, columns],
            out_sems.at[len(stores)],
        )
        made.start()
        stores.append(made)

    earlier = list(sent)
    sent.clear()
    last = gather(residuals, here, SETS, second_send, second_recv, sent, keep)
    next(last)
    for made in earlier:
        made.wait_send()
    for _ in last:
        pass

    acc[...] = jnp.zeros_like(acc)

    @pl.loop(0, GROUP)
    def _(spot):
        acc[...] += lax.dot_general(
            residuals[lax.div(spot, 4), lax.rem(spot, 4)].reshape(TOKENS, 2 * WIDE),
            weights_down[spot],
            (((1,), (1,)), ((), ())),
            preferred_element_type=F32,
        )

    for k in range(4):
        span = slice(k * 128, (k + 1) * 128)
        back_dot, back_grad = acc[span, :PAD], acc[span, PAD:]
        slopes = slopes_ref[span]
        grad_pre = (back_grad * slopes).T.astype(BF16)
        grad_pre_dot = (back_dot * slopes + back_grad * bend_ref[span]).T.astype(BF16)
        grads_t[0:PAD, span] = grad_pre
        grads_t[PAD:, span] = grad_pre_dot

    for made in stores:
        made.wait()
    for made in sent:
        made.wait_send()


def update(
    grads_t,
    both_t,
    tokens,
    residuals,
    tangent_up,
    tangent_down,
    moment_up,
    moment_down,
    curve_up,
    curve_down,
    step_up,
    step_down,
    moment_up_next,
    moment_down_next,
    curve_up_next,
    curve_down_next,
):
    first = 2 * pl.program_id(0)
    loss_scale = 1.0 / math.sqrt(TOKENS)
    wide = [tokens[first + k].reshape(TOKENS, WIDE) for k in range(2)]
    up = jnp.dot(grads_t[...], jnp.concatenate(wide, axis=1), preferred_element_type=F32)
    step_up[...], moment_up_next[...], curve_up_next[...] = refresh(
        moment_up[...],
        curve_up[...],
        loss_scale * up[:HID],
        loss_scale * up[PAD : PAD + HID],
        tangent_up[...],
    )
    grad, hvp = [], []
    for k in range(2):
        down = jnp.dot(
            both_t[...],
            residuals[first + k].reshape(TOKENS, 2 * WIDE),
            preferred_element_type=F32,
        )
        grad.append(down[:HID, WIDE:])
        hvp.append(down[:HID, :WIDE] + down[PAD : PAD + HID, WIDE:])
    step_down[...], moment_down_next[...], curve_down_next[...] = refresh(
        moment_down[...],
        curve_down[...],
        loss_scale * jnp.concatenate(grad, axis=1),
        loss_scale * jnp.concatenate(hvp, axis=1),
        tangent_down[...],
    )


def per_device(
    tokens,
    target,
    master_up,
    master_down,
    tangent_up,
    tangent_down,
    moment_up,
    moment_down,
    curve_up,
    curve_down,
):
    wide32 = jax.ShapeDtypeStruct((HID, D), F32)
    wide16 = jax.ShapeDtypeStruct((HID, D), BF16)
    blocks = (4, 4, 8, 16)
    any_spec = pl.BlockSpec(memory_space=pl.ANY)
    vmem_spec = pl.BlockSpec(memory_space=pltpu.VMEM)
    scratch = [pltpu.VMEM((2, D), BF16)] * 2
    scratch += [pltpu.VMEM((HID, D), F32)] * 2 + [pltpu.VMEM((HID, D), BF16)] * 2
    scratch += [
        pltpu.VMEM((GROUP, 16, WIDE), BF16),
        pltpu.VMEM((2,) + blocks + (WIDE,), BF16),
        pltpu.VMEM((GROUP, 4, 8, 16, WIDE), BF16),
        pltpu.VMEM((4, 2 * PAD, 768), BF16),
        pltpu.VMEM((GROUP, 2 * PAD, 2 * WIDE), BF16),
        pltpu.VMEM((TOKENS, 2 * PAD), F32),
        pltpu.VMEM((4, 8, 16, 2 * PAD), BF16),
        pltpu.VMEM((TOKENS, PAD), F32),
        pltpu.VMEM((TOKENS, PAD), F32),
        pltpu.VMEM((2, 4, 4, 4, 16, 2 * WIDE), BF16),
        pltpu.VMEM((2, 4, 4, 4, 16, 2 * WIDE), BF16),
        pltpu.VMEM(blocks + (2 * WIDE,), BF16),
        pltpu.VMEM((2,) + blocks + (2 * WIDE,), BF16),
        pltpu.VMEM((3, 4, 8, 16, MAIN), BF16),
        pltpu.VMEM((3, 8, 16, MAIN), BF16),
        pltpu.VMEM((7, 16, MAIN), BF16),
        pltpu.VMEM((7, 4, 4, 16, 2 * WIDE - MAIN), BF16),
        pltpu.VMEM((3, 4, 16, 2 * WIDE - MAIN), BF16),
        pltpu.VMEM((3, 16, 2 * WIDE - MAIN), BF16),
    ]
    dma = pltpu.SemaphoreType.DMA
    scratch += [
        dma((6,)),
        dma((11,)),
        dma((2, 4)),
        dma((2, 4)),
        dma((GROUP,)),
        dma((GROUP,)),
        dma((GATHER_COUNT,)),
        dma((GATHER_COUNT,)),
        dma((SCATTER_COUNT,)),
        dma((SCATTER_COUNT,)),
        dma((GATHER_COUNT,)),
        dma((GATHER_COUNT,)),
    ]
    all_tokens, residuals, both_t, grads_t = pl.pallas_call(
        kernel,
        out_shape=(
            pltpu.VMEM((GROUP, 4, 8, 16, WIDE), BF16),
            pltpu.VMEM((2,) + blocks + (2 * WIDE,), BF16),
            pltpu.VMEM((2 * PAD, TOKENS), BF16),
            pltpu.VMEM((2 * PAD, TOKENS), BF16),
        ),
        in_specs=[any_spec] * 6,
        out_specs=(vmem_spec,) * 4,
        scratch_shapes=scratch,
        compiler_params=pltpu.CompilerParams(
            collective_id=0, has_side_effects=True, vmem_limit_bytes=49 * 1024 * 1024
        ),
        cost_estimate=pl.CostEstimate(
            flops=3_000_000_000, bytes_accessed=16_000_000, transcendentals=131072
        ),
    )(tokens, target, master_up, master_down, tangent_up, tangent_down)
    residuals = residuals.reshape((GROUP, 4, 8, 16, 2 * WIDE))
    whole = pl.BlockSpec((2 * PAD, TOKENS), lambda spot: (0, 0))
    part = pl.BlockSpec((HID, 2 * WIDE), lambda spot: (0, spot))
    return pl.pallas_call(
        update,
        grid=(GROUP // 2,),
        out_shape=(wide32, wide32, wide16, wide16, wide16, wide16),
        in_specs=[
            whole,
            whole,
            vmem_spec,
            vmem_spec,
        ]
        + [part] * 6,
        out_specs=(part,) * 6,
        compiler_params=pltpu.CompilerParams(vmem_limit_bytes=30 * 1024 * 1024),
        cost_estimate=pl.CostEstimate(
            flops=1_500_000_000, bytes_accessed=18_000_000, transcendentals=0
        ),
    )(
        grads_t,
        both_t,
        all_tokens,
        residuals,
        tangent_up,
        tangent_down,
        moment_up,
        moment_down,
        curve_up,
        curve_down,
    )


def solution(mesh):
    rows = P(("dp", "tensor"), None)
    return jax.shard_map(
        per_device, mesh=mesh, in_specs=(rows,) * 10, out_specs=(rows,) * 6, check_vma=False
    )
```
